32 devices in a mesh: flow: 8 (over z, x), shear: 4 (over y, core).
Axes of the slice: x: 2, y: 2, z: 4, core: 2. Of those that a mesh axis runs over, the one named last changes fastest.
Arguments:
- populations: float32 [19, 8, 128, 512], P(None, None, 'flow', 'shear'), may hold values from 0.5 to 2
- le_cells: int32 [2], replicated, may hold values from 0 to 127
- le_weight: int32 [2], replicated, may hold values from 0 to 255
Outputs:
- result: float32 [19, 8, 128, 512], P(None, None, 'flow', 'shear')
The draws below stay inside these ranges and needn't reach their ends.
Inputs may be any that keep to these rules, and one draw needn't show every extreme that they name: `le_cells`: offset in whole cells, any value in the range. `le_weight`: fraction numerator, any value in the range.
All inputs are finite; a program needn't handle non-finite values.
Results may differ from the reference program's by a relative error of at most 0.0001.
Values sent between devices are 32-bit elements; how exact they have to be, the bound alone decides.
No kernel may reach another device: no remote copies, remote signals or barrier semaphores. Data moves between devices by JAX's collectives and lax.ppermute only.
A program may use at most 64 MiB of HBM per device.

```python
import jax
import jax.numpy as jnp
import numpy as np

NZ = 8
STEPS = 2
WEIGHT_DENOM = 256
NX = 128
NY = 512


def block_levels(key, dims, pieces, smallest, largest):
    def one(axis_at, shards_of):
        draws = jax.random.uniform(jax.random.fold_in(jax.random.fold_in(key, 6), axis_at), (shards_of,), jnp.float32, smallest / len(pieces), largest / len(pieces))
        return jnp.repeat(jnp.exp(draws), dims[axis_at] // shards_of).reshape((-1,) + (1,) * (len(dims) - axis_at - 1))

    level = one(*pieces[0])
    for cut in pieces[1:]:
        level = level * one(*cut)
    return level


def setup_inputs(seed: int = 0) -> dict:
    key_list = jax.random.split(jax.random.key(seed), 4)
    populations = jnp.clip(0.5 + 1.5 * jax.random.uniform(key_list[0], (19, NZ, NX, NY), jnp.float32) ** block_levels(key_list[0], (19, NZ, NX, NY), ((2, 8), (3, 4)), -0.2, 0.2), 0.5, 2.0)
    le_cells = jax.random.randint(key_list[1], (STEPS,), 0, NX).astype(jnp.int32)
    le_weight = jax.random.randint(key_list[2], (STEPS,), 0, WEIGHT_DENOM).astype(jnp.int32)
    return dict(populations=populations, le_cells=le_cells, le_weight=le_weight)


VELOCITY = [(0, 0, 0), (1, 0, 0), (-1, 0, 0), (0, 1, 0), (0, -1, 0), (0, 0, 1), (0, 0, -1),
            (1, 1, 0), (-1, -1, 0), (1, -1, 0), (-1, 1, 0), (1, 0, 1), (-1, 0, -1), (1, 0, -1),
            (-1, 0, 1), (0, 1, 1), (0, -1, -1), (0, 1, -1), (0, -1, 1)]
WEIGHTS = [1.0 / 3.0] + [1.0 / 18.0] * 6 + [1.0 / 36.0] * 12
EASTWARD = np.array([1, 7, 9, 11, 13])
WESTWARD = np.array([2, 8, 10, 12, 14])
UPWARD = np.array([3, 7, 10, 15, 17])
DOWNWARD = np.array([4, 8, 9, 16, 18])
RISING = np.array([5, 11, 14, 15, 18])
FALLING = np.array([6, 12, 13, 16, 17])
RELAX_TIME = 0.6
WALL_SPEED = 0.1


def collide(lattice):
    density = jnp.sum(lattice, axis=0)
    flux_x = jnp.sum(lattice[EASTWARD], axis=0) - jnp.sum(lattice[WESTWARD], axis=0)
    flux_y = jnp.sum(lattice[UPWARD], axis=0) - jnp.sum(lattice[DOWNWARD], axis=0)
    flux_z = jnp.sum(lattice[RISING], axis=0) - jnp.sum(lattice[FALLING], axis=0)
    speed_x = flux_x / density
    speed_y = flux_y / density
    speed_z = flux_z / density
    square = speed_x * speed_x + speed_y * speed_y + speed_z * speed_z
    relaxed = []
    for lane_id in range(19):
        move_x, move_y, move_z = VELOCITY[lane_id]
        along = move_x * speed_x + move_y * speed_y + move_z * speed_z
        balance = WEIGHTS[lane_id] * density * (1.0 + 3.0 * along + 4.5 * along * along - 1.5 * square)
        relaxed.append(lattice[lane_id] - (lattice[lane_id] - balance) / RELAX_TIME)
    return jnp.stack(relaxed), density


def boost(pops, rho, push, lanes):
    factor = jnp.array([3.0 * WEIGHTS[int(k)] * VELOCITY[int(k)][0] for k in lanes], jnp.float32)
    return pops + factor[:, None, None] * (rho * push)[None]


def extend(relaxed, low_pops, high_pops):
    shape = relaxed.shape
    ext = jnp.zeros((shape[0], shape[1], shape[2], shape[3] + 2), jnp.float32)
    ext = ext.at[:, :, :, 1:-1].set(relaxed)
    ext = ext.at[UPWARD, :, :, 0].set(low_pops)
    ext = ext.at[DOWNWARD, :, :, -1].set(high_pops)
    return ext


def stream(padded, width_x, width_y):
    moved = []
    for lane_id in range(19):
        move_x, move_y, move_z = VELOCITY[lane_id]
        window_part = padded[lane_id, :, 1 - move_x:1 - move_x + width_x, 1 - move_y:1 - move_y + width_y]
        moved.append(jnp.roll(window_part, move_z, axis=0))
    return jnp.stack(moved)


def reference(populations, le_cells, le_weight):
    lattice = populations
    width_x = lattice.shape[2]
    width_y = lattice.shape[3]
    for turn in range(STEPS):
        relaxed, density = collide(lattice)
        offset_cells = le_cells[turn]
        fraction = le_weight[turn].astype(jnp.float32) / WEIGHT_DENOM
        upper_row = jnp.concatenate([relaxed[UPWARD][..., width_y - 1], density[None, :, :, width_y - 1]], 0)
        lower_row = jnp.concatenate([relaxed[DOWNWARD][..., 0], density[None, :, :, 0]], 0)
        below = (1.0 - fraction) * jnp.roll(upper_row, -offset_cells, axis=2) + fraction * jnp.roll(upper_row, -offset_cells - 1, axis=2)
        above = fraction * jnp.roll(lower_row, offset_cells + 1, axis=2) + (1.0 - fraction) * jnp.roll(lower_row, offset_cells, axis=2)
        low_pops = boost(below[:5], below[5], jnp.float32(-WALL_SPEED), UPWARD)
        high_pops = boost(above[:5], above[5], jnp.float32(WALL_SPEED), DOWNWARD)
        ext = extend(relaxed, low_pops, high_pops)
        padded = jnp.concatenate([ext[:, :, -1:], ext, ext[:, :, :1]], axis=2)
        lattice = stream(padded, width_x, width_y)
    return lattice
```

```python
import jax
import jax.numpy as jnp
from jax import lax
from jax.experimental import pallas as pl
from jax.experimental.pallas import tpu as pltpu
from jax.sharding import PartitionSpec as P

WEIGHT_DENOM = 256
VELOCITY = [
    (0, 0, 0),
    (1, 0, 0),
    (-1, 0, 0),
    (0, 1, 0),
    (0, -1, 0),
    (0, 0, 1),
    (0, 0, -1),
    (1, 1, 0),
    (-1, -1, 0),
    (1, -1, 0),
    (-1, 1, 0),
    (1, 0, 1),
    (-1, 0, -1),
    (1, 0, -1),
    (-1, 0, 1),
    (0, 1, 1),
    (0, -1, -1),
    (0, 1, -1),
    (0, -1, 1),
]
WEIGHTS = [1.0 / 3.0] + [1.0 / 18.0] * 6 + [1.0 / 36.0] * 12
EAST = [1, 7, 9, 11, 13]
WEST = [2, 8, 10, 12, 14]
UP = [3, 7, 10, 15, 17]
DOWN = [4, 8, 9, 16, 18]
OMEGA = 1.0 / 0.6
WALL_SPEED = 0.1
BOOST = 3.0 * WALL_SPEED / 36.0
NZ = 8
LANES = 128
GAP = 4
HALF = 64
BASE = 2


def lane_iota():
    return lax.broadcasted_iota(jnp.int32, (NZ, LANES), 1)


def roll_y(v, by):
    by = by % LANES
    return pltpu.roll(v, by, 1) if by else v


def roll_z(v, by):
    by = by % NZ
    return pltpu.roll(v, by, 0) if by else v


def moments(f):
    e = f[1] + f[11] + f[13]
    w = f[2] + f[12] + f[14]
    n = f[3] + f[15] + f[17]
    s = f[4] + f[16] + f[18]
    d79 = f[7] + f[9]
    d810 = f[8] + f[10]
    rho = ((f[0] + f[5]) + f[6]) + (e + w) + (n + s) + (d79 + d810)
    jx = (e - w) + (d79 - d810)
    jy = (n - s) + ((f[7] - f[9]) + (f[10] - f[8]))
    jz = (f[5] - f[6]) + ((f[11] - f[12]) + (f[14] - f[13])) + ((f[15] - f[16]) + (f[18] - f[17]))
    return rho, jx, jy, jz


def relax(rho, jx, jy, jz, f, wanted):
    inv = 1.0 / rho
    ux, uy, uz = jx * inv, jy * inv, jz * inv
    base = (rho - 1.5 * (jx * ux + jy * uy + jz * uz)) * (OMEGA / 36.0)
    keep = 1.0 - OMEGA
    post = {}
    done = set()
    for q in wanted:
        if q in done:
            continue
        cx, cy, cz = VELOCITY[q]
        if q == 0:
            post[0] = keep * f[0] + 12.0 * base
            continue
        opposite = VELOCITY.index((-cx, -cy, -cz))
        jc, uc = None, None
        for c, j, u in ((cx, jx, ux), (cy, jy, uy), (cz, jz, uz)):
            if c:
                if jc is None:
                    jc, uc = (j, u) if c > 0 else (-j, -u)
                else:
                    jc, uc = (jc + j, uc + u) if c > 0 else (jc - j, uc - u)
        scale = WEIGHTS[q] * 36.0
        even = base * scale if scale != 1.0 else base
        even = even + (jc * uc) * (4.5 * OMEGA * WEIGHTS[q])
        odd = jc * (3.0 * OMEGA * WEIGHTS[q])
        post[q] = keep * f[q] + (even + odd)
        done.add(q)
        if opposite in wanted:
            post[opposite] = keep * f[opposite] + (even - odd)
            done.add(opposite)
    return post


def classes(p, across):
    if across == "x":
        plus, minus = (1, 11, 13), (2, 12, 14)
    else:
        plus, minus = (3, 15, 17), (4, 16, 18)
    rising, falling = plus[1], plus[2]
    low, high = minus[1], minus[2]
    return [
        p[0] + p[5] + p[6],
        p[plus[0]] + p[rising] + p[falling],
        p[minus[0]] + p[low] + p[high],
        p[5] - p[6],
        p[rising] - p[falling],
        p[high] - p[low],
    ]


def column(ref, q, x, width):
    return ref[q, pl.ds(x, NZ, stride=width), :]


def pack_kernel(flows, shears, width, f_hbm, rows_ref, east_ref, west_ref, f_ref, sems):
    copies = [pltpu.make_async_copy(f_hbm.at[q], f_ref.at[q], sems.at[q]) for q in range(19)]
    for copy in copies:
        copy.start()
    shear = lax.axis_index("shear")
    lane = lane_iota()
    boost_up = jnp.where(shear == shears - 1, -BOOST, 0.0).astype(jnp.float32)
    boost_down = jnp.where(shear == 0, BOOST, 0.0).astype(jnp.float32)
    here = [(lane >= x * GAP) & (lane < (x + 1) * GAP) for x in range(width)]
    edge = []
    for q in range(19):
        copies[q].wait()
        total = jnp.ones((NZ, LANES), jnp.float32)
        for x in range(width):
            total = jnp.where(here[x], roll_y(column(f_ref, q, x, width), x * GAP + 2), total)
        edge.append(total)
    rho, jx, jy, jz = moments(edge)
    post = relax(rho, jx, jy, jz, edge, range(19))
    post = {q: roll_z(post[q], VELOCITY[q][2]) for q in range(19)}
    sums = classes(post, "x")

    def groups(ghosts, outer, at, far):
        planes = [(g, at) for g in ghosts] + [(s, at) for s in sums] + [(o, far) for o in outer]
        vregs = []
        for v in range(2):
            total = None
            for half in range(2):
                for slot in range(GAP):
                    plane, row = planes[(v * 2 + half) * GAP + slot]
                    moved = roll_y(plane, half * HALF + slot - row)
                    if total is None:
                        total = moved
                    else:
                        inside = (lane >= half * HALF) & (lane < (half + 1) * HALF)
                        total = jnp.where(inside & (lane % GAP == slot), moved, total)
            vregs.append(total)
        return vregs

    ups = [post[q] + VELOCITY[q][0] * boost_up * rho if VELOCITY[q][0] else post[q] for q in UP]
    downs = [post[q] + VELOCITY[q][0] * boost_down * rho if VELOCITY[q][0] else post[q] for q in DOWN]
    up0, up1 = groups(ups, [post[q] for q in UP], 1, 0)
    down0, down1 = groups(downs, [post[q] for q in DOWN], 2, 3)
    above = lax.rem(shear + 1, shears)
    below = lax.rem(shear + shears - 1, shears)

    def put(at):
        for to, first, second in ((above, up0, up1), (below, down0, down1), (shear, up0, down0)):
            rows_ref[at * shears + to, 0:NZ, :] = first
            rows_ref[at * shears + to, NZ : 2 * NZ, :] = second
        for extra in range(2, shears - 1):
            rows_ref[at * shears + lax.rem(shear + extra, shears)] = jnp.zeros((2 * NZ, LANES), jnp.float32)

    if flows <= 8:
        for at in range(flows):
            put(at)
    else:
        pl.loop(0, flows)(put)

    for out, near, far, lanes in ((east_ref, width - 1, width - 2, EAST), (west_ref, 0, 1, WEST)):
        for at, first in ((far, 0), (near, 5)):
            f = [column(f_ref, q, at, width) for q in range(19)]
            wanted = list(range(19)) if at == near else lanes
            post = relax(*moments(f), f, wanted)
            for q in wanted:
                post[q] = roll_y(roll_z(post[q], VELOCITY[q][2]), VELOCITY[q][1])
            for i, q in enumerate(lanes):
                out[first + i] = post[q]
            if at == near:
                for i, s in enumerate(classes(post, "y")):
                    out[10 + i] = s


def local_kernel(width, f_ref, a_ref):
    def step(x):
        f = [column(f_ref, q, x, width) for q in range(19)]
        post = relax(*moments(f), f, range(19))
        for q in range(19):
            cx, cy, cz = VELOCITY[q]
            a_ref[q, x + 1 + cx] = roll_y(roll_z(post[q], cz), cy)

    pl.loop(0, width, unroll=2)(step)
    for q in range(19):
        cx = VELOCITY[q][0]
        zero = jnp.zeros((NZ, LANES), jnp.float32)
        for x in (0, 1, width, width + 1):
            if not 0 <= x - 1 - cx < width:
                a_ref[q, x] = zero


def finish_kernel(
    flows, shears, width, cells, weight, a_hbm, rows_ref, west_ref, east_ref, out_hbm,
    a_ref, out_ref, sem_in, sem_out,
):
    load = pltpu.make_async_copy(a_hbm, a_ref, sem_in)
    load.start()
    flow = lax.axis_index("flow")
    shear = lax.axis_index("shear")
    lane = lane_iota()
    total_x = flows * width
    at_bottom = shear == 0
    at_top = shear == shears - 1
    above = lax.rem(shear + 1, shears)
    below = lax.rem(shear + shears - 1, shears)
    k1, k2 = cells[0], cells[1]
    frac = [weight[s].astype(jnp.float32) / WEIGHT_DENOM for s in range(2)]
    one, zero = jnp.float32(1.0), jnp.float32(0.0)

    def window(start, source, vreg, half):
        first = lax.rem(flow * width + start - BASE + 2 * total_x, total_x)
        block = lax.div(first, width)
        skip = (first - block * width) * GAP
        a, b, c = [
            rows_ref[lax.rem(block + k, flows) * shears + source, vreg * NZ : (vreg + 1) * NZ, :]
            for k in range(3)
        ]
        if half:
            a, c = roll_y(a, HALF), roll_y(c, HALF)
        else:
            b = roll_y(b, HALF)
        both = jnp.where(lane < HALF, a, b)
        return pltpu.roll(jnp.where(lane >= skip, both, c), lax.rem(LANES - skip, LANES), 1)

    def side(upward):
        lanes = UP if upward else DOWN
        others = DOWN if upward else UP
        active = at_bottom if upward else at_top
        source = below if upward else above

        def starts(k, low):
            return k if low else -k - 1

        def coefs(s, low):
            pair = (one - frac[s], frac[s]) if low else (frac[s], one - frac[s])
            return jnp.where(active, pair[0], one), jnp.where(active, pair[1], zero)

        def mixed(v, pair):
            return pair[0] * v + pair[1] * roll_y(v, -GAP)

        start1 = jnp.where(active, starts(k1, upward), 0)
        start2 = jnp.where(active, starts(k2, upward), 0)
        start3 = jnp.where(active, starts(k2, upward) + starts(k1, not upward), 0)
        near = [mixed(window(start1, source, 0, h), coefs(0, upward)) for h in range(2)]
        ghost1 = {q: (near[i // GAP], i % GAP) for i, q in enumerate(lanes)}
        packs = [None] + [window(start2, source, v, h) for v, h in ((0, 1), (1, 0), (1, 1))]
        pair3 = coefs(0, not upward)
        own = 1 if upward else 0
        back = [mixed(window(start3, shear, own, h), pair3) for h in range(2)]

        def plane(at, by):
            return roll_y(packs[at // GAP], by * GAP - at % GAP)

        f = {}
        for i, q in enumerate(lanes):
            f[q] = plane(11 + i, VELOCITY[q][0])
        for i, q in enumerate(others):
            f[q] = roll_y(back[i // GAP], VELOCITY[q][0] * GAP - i % GAP)
        mid, plus, minus = plane(5, 0), plane(6, 1), plane(7, -1)
        midz, plusz, minusz = plane(8, 0), plane(9, 1), plane(10, -1)
        up = [f[q] for q in UP]
        down = [f[q] for q in DOWN]
        sum_up = up[0] + up[1] + up[2] + up[3] + up[4]
        sum_down = down[0] + down[1] + down[2] + down[3] + down[4]
        rho = (mid + plus + minus) + (sum_up + sum_down)
        jx = (plus - minus) + ((f[7] - f[10]) + (f[9] - f[8]))
        jy = sum_up - sum_down
        jz = (midz + plusz + minusz) + ((f[15] - f[17]) + (f[18] - f[16]))
        post = relax(rho, jx, jy, jz, f, lanes)
        boost = jnp.where(active, -BOOST if upward else BOOST, 0.0).astype(jnp.float32)
        pair2 = coefs(1, upward)
        ghost2 = {}
        for q in lanes:
            cx, _, cz = VELOCITY[q]
            p = post[q] + cx * boost * rho if cx else post[q]
            ghost2[q] = (roll_z(mixed(p, pair2), cz), 0)
        return ghost1, ghost2

    up1, up2 = side(True)
    down1, down2 = side(False)
    ghosts1 = {**up1, **down1}
    ghosts2 = {**up2, **down2}
    at_first = lane == 0
    at_last = lane == LANES - 1

    def insert(v, ghosts, q, x):
        cy = VELOCITY[q][1]
        if cy == 0:
            return v
        g, slot = ghosts[q]
        by = (0 if cy > 0 else LANES - 1) - ((x + BASE) * GAP + slot)
        if isinstance(x, int):
            moved = roll_y(g, by)
        else:
            moved = pltpu.roll(g, lax.rem(by + LANES, LANES), 1)
        return jnp.where(at_first if cy > 0 else at_last, moved, v)

    load.wait()
    for i in range(5):
        a_ref[EAST[i], 1] = west_ref[5 + i]
        a_ref[WEST[i], width] = east_ref[5 + i]

    def put(q, x, post):
        cx, cy, cz = VELOCITY[q]
        v = insert(roll_y(roll_z(post[q], cz), cy), ghosts2, q, x)
        out_ref[q, pl.ds(x + cx, NZ, stride=width), :] = v

    def inner(x, keep):
        f = [insert(a_ref[q, x + 1], ghosts1, q, x - VELOCITY[q][0]) for q in range(19)]
        wanted = [q for q in range(19) if VELOCITY[q][0] != -keep or keep == 0]
        post = relax(*moments(f), f, wanted)
        for q in wanted:
            put(q, x, post)

    for x, halo, entering, leaving in ((-1, west_ref, EAST, WEST), (width, east_ref, WEST, EAST)):
        cx = VELOCITY[entering[0]][0]
        f = {q: insert(halo[i], ghosts1, q, x - cx) for i, q in enumerate(entering)}
        for q in leaving:
            f[q] = insert(a_ref[q, x + 1], ghosts1, q, x + cx)

        def edge_value(q):
            g, slot = ghosts1[q]
            return roll_y(g, (0 if VELOCITY[q][1] > 0 else LANES - 1) - ((x + BASE) * GAP + slot))

        n, np_, nm = edge_value(3), edge_value(15), edge_value(17)
        s, sm, sp = edge_value(4), edge_value(16), edge_value(18)
        plus = jnp.where(at_first, n + np_ + nm, halo[11])
        minus = jnp.where(at_last, s + sm + sp, halo[12])
        plusz = jnp.where(at_first, np_ - nm, halo[14])
        minusz = jnp.where(at_last, sp - sm, halo[15])
        sum_e = f[1] + f[7] + f[9] + f[11] + f[13]
        sum_w = f[2] + f[8] + f[10] + f[12] + f[14]
        rho = (halo[10] + plus + minus) + (sum_e + sum_w)
        jx = sum_e - sum_w
        jy = (plus - minus) + ((f[7] - f[8]) + (f[10] - f[9]))
        jz = (halo[13] + plusz + minusz) + ((f[11] - f[12]) + (f[14] - f[13]))
        post = relax(rho, jx, jy, jz, f, entering)
        for q in entering:
            put(q, x, post)

    inner(0, 1)
    pl.loop(1, width - 1, unroll=2)(lambda x: inner(x, 0))
    inner(width - 1, -1)
    store = pltpu.make_async_copy(out_ref, out_hbm, sem_out)
    store.start()
    store.wait()


def per_device(populations, le_cells, le_weight):
    width = populations.shape[2]
    height = populations.shape[3]
    flows = lax.axis_size("flow")
    shears = lax.axis_size("shear")
    assert populations.shape[:2] == (19, NZ) and height == LANES
    assert width * GAP == HALF and shears >= 3 and flows >= 3
    f32 = jnp.float32
    f = populations.reshape(19, NZ * width, height)
    vmem = pl.BlockSpec(memory_space=pltpu.VMEM)
    anyspace = pl.BlockSpec(memory_space=pl.ANY)
    smem = pl.BlockSpec(memory_space=pltpu.SMEM)
    params = pltpu.CompilerParams(vmem_limit_bytes=32 * 1024 * 1024)
    devices = flows * shears

    def body(kernel, *fixed):
        return lambda *refs: kernel(*fixed, *refs)

    rows, east, west = pl.pallas_call(
        body(pack_kernel, flows, shears, width),
        out_shape=[
            jax.ShapeDtypeStruct((devices, 2 * NZ, LANES), f32),
            jax.ShapeDtypeStruct((16, NZ, LANES), f32),
            jax.ShapeDtypeStruct((16, NZ, LANES), f32),
        ],
        in_specs=[anyspace],
        out_specs=[vmem] * 3,
        scratch_shapes=[pltpu.VMEM((19, NZ * width, LANES), f32), pltpu.SemaphoreType.DMA((19,))],
        compiler_params=params,
        name="pack",
    )(f)
    rows = lax.all_to_all(rows, ("flow", "shear"), 0, 0, tiled=True)
    from_west = lax.ppermute(east, "flow", [(i, (i + 1) % flows) for i in range(flows)])
    from_east = lax.ppermute(west, "flow", [(i, (i - 1) % flows) for i in range(flows)])
    streamed = pl.pallas_call(
        body(local_kernel, width),
        out_shape=jax.ShapeDtypeStruct((19, width + 2, NZ, LANES), f32),
        in_specs=[vmem],
        out_specs=vmem,
        compiler_params=params,
        cost_estimate=pl.CostEstimate(flops=8_000_000, bytes_accessed=2_700_000, transcendentals=0),
        name="local",
    )(f)
    out = pl.pallas_call(
        body(finish_kernel, flows, shears, width),
        out_shape=jax.ShapeDtypeStruct((19, NZ * width, LANES), f32),
        in_specs=[smem, smem, anyspace, vmem, vmem, vmem],
        out_specs=anyspace,
        scratch_shapes=[
            pltpu.VMEM((19, width + 2, NZ, LANES), f32),
            pltpu.VMEM((19, NZ * width, LANES), f32),
            pltpu.SemaphoreType.DMA,
            pltpu.SemaphoreType.DMA,
        ],
        compiler_params=params,
        name="finish",
    )(le_cells, le_weight, streamed, rows, from_west, from_east)
    return out.reshape(populations.shape)


def solution(mesh):
    return jax.shard_map(
        per_device,
        mesh=mesh,
        in_specs=(P(None, None, "flow", "shear"), P(), P()),
        out_specs=P(None, None, "flow", "shear"),
        check_vma=False,
    )
```

```python
import jax
import jax.numpy as jnp
from jax import lax
from jax.experimental import pallas as pl
from jax.experimental.pallas import tpu as pltpu
from jax.sharding import PartitionSpec as P

WEIGHT_DENOM = 256
VELOCITY = [
    (0, 0, 0),
    (1, 0, 0),
    (-1, 0, 0),
    (0, 1, 0),
    (0, -1, 0),
    (0, 0, 1),
    (0, 0, -1),
    (1, 1, 0),
    (-1, -1, 0),
    (1, -1, 0),
    (-1, 1, 0),
    (1, 0, 1),
    (-1, 0, -1),
    (1, 0, -1),
    (-1, 0, 1),
    (0, 1, 1),
    (0, -1, -1),
    (0, 1, -1),
    (0, -1, 1),
]
WEIGHTS = [1.0 / 3.0] + [1.0 / 18.0] * 6 + [1.0 / 36.0] * 12
EAST = [1, 7, 9, 11, 13]
WEST = [2, 8, 10, 12, 14]
UP = [3, 7, 10, 15, 17]
DOWN = [4, 8, 9, 16, 18]
OMEGA = 1.0 / 0.6
WALL_SPEED = 0.1
BOOST = 3.0 * WALL_SPEED / 36.0
NZ = 8
LANES = 128
GAP = 4
HALF = 64
BASE = 2


def lane_iota():
    return lax.broadcasted_iota(jnp.int32, (NZ, LANES), 1)


def roll_y(v, by):
    by = by % LANES
    return pltpu.roll(v, by, 1) if by else v


def roll_z(v, by):
    by = by % NZ
    return pltpu.roll(v, by, 0) if by else v


def moments(f):
    e = f[1] + f[11] + f[13]
    w = f[2] + f[12] + f[14]
    n = f[3] + f[15] + f[17]
    s = f[4] + f[16] + f[18]
    d79 = f[7] + f[9]
    d810 = f[8] + f[10]
    rho = ((f[0] + f[5]) + f[6]) + (e + w) + (n + s) + (d79 + d810)
    jx = (e - w) + (d79 - d810)
    jy = (n - s) + ((f[7] - f[9]) + (f[10] - f[8]))
    jz = (f[5] - f[6]) + ((f[11] - f[12]) + (f[14] - f[13])) + ((f[15] - f[16]) + (f[18] - f[17]))
    return rho, jx, jy, jz


def relax(rho, jx, jy, jz, f, wanted):
    inv = 1.0 / rho
    ux, uy, uz = jx * inv, jy * inv, jz * inv
    base = (rho - 1.5 * (jx * ux + jy * uy + jz * uz)) * (OMEGA / 36.0)
    keep = 1.0 - OMEGA
    post = {}
    done = set()
    for q in wanted:
        if q in done:
            continue
        cx, cy, cz = VELOCITY[q]
        if q == 0:
            post[0] = keep * f[0] + 12.0 * base
            continue
        opposite = VELOCITY.index((-cx, -cy, -cz))
        jc, uc = None, None
        for c, j, u in ((cx, jx, ux), (cy, jy, uy), (cz, jz, uz)):
            if c:
                if jc is None:
                    jc, uc = (j, u) if c > 0 else (-j, -u)
                else:
                    jc, uc = (jc + j, uc + u) if c > 0 else (jc - j, uc - u)
        scale = WEIGHTS[q] * 36.0
        even = base * scale if scale != 1.0 else base
        even = even + (jc * uc) * (4.5 * OMEGA * WEIGHTS[q])
        odd = jc * (3.0 * OMEGA * WEIGHTS[q])
        post[q] = keep * f[q] + (even + odd)
        done.add(q)
        if opposite in wanted:
            post[opposite] = keep * f[opposite] + (even - odd)
            done.add(opposite)
    return post


def classes(p, across):
    if across == "x":
        plus, minus = (1, 11, 13), (2, 12, 14)
    else:
        plus, minus = (3, 15, 17), (4, 16, 18)
    rising, falling = plus[1], plus[2]
    low, high = minus[1], minus[2]
    return [
        p[0] + p[5] + p[6],
        p[plus[0]] + p[rising] + p[falling],
        p[minus[0]] + p[low] + p[high],
        p[5] - p[6],
        p[rising] - p[falling],
        p[high] - p[low],
    ]


def column(ref, q, x, width):
    return ref[q, pl.ds(x, NZ, stride=width), :]


def pack_kernel(flows, shears, width, f_ref, rows_ref, east_ref, west_ref):
    shear = lax.axis_index("shear")
    lane = lane_iota()
    boost_up = jnp.where(shear == shears - 1, -BOOST, 0.0).astype(jnp.float32)
    boost_down = jnp.where(shear == 0, BOOST, 0.0).astype(jnp.float32)
    here = [(lane >= x * GAP) & (lane < (x + 1) * GAP) for x in range(width)]
    edge = []
    for q in range(19):
        total = jnp.ones((NZ, LANES), jnp.float32)
        for x in range(width):
            total = jnp.where(here[x], roll_y(column(f_ref, q, x, width), x * GAP + 2), total)
        edge.append(total)
    rho, jx, jy, jz = moments(edge)
    post = relax(rho, jx, jy, jz, edge, range(19))
    post = {q: roll_z(post[q], VELOCITY[q][2]) for q in range(19)}
    sums = classes(post, "x")

    def groups(ghosts, outer, at, far):
        planes = [(g, at) for g in ghosts] + [(s, at) for s in sums] + [(o, far) for o in outer]
        vregs = []
        for v in range(2):
            total = None
            for half in range(2):
                for slot in range(GAP):
                    plane, row = planes[(v * 2 + half) * GAP + slot]
                    moved = roll_y(plane, half * HALF + slot - row)
                    if total is None:
                        total = moved
                    else:
                        inside = (lane >= half * HALF) & (lane < (half + 1) * HALF)
                        total = jnp.where(inside & (lane % GAP == slot), moved, total)
            vregs.append(total)
        return vregs

    ups = [post[q] + VELOCITY[q][0] * boost_up * rho if VELOCITY[q][0] else post[q] for q in UP]
    downs = [post[q] + VELOCITY[q][0] * boost_down * rho if VELOCITY[q][0] else post[q] for q in DOWN]
    up0, up1 = groups(ups, [post[q] for q in UP], 1, 0)
    down0, down1 = groups(downs, [post[q] for q in DOWN], 2, 3)
    above = lax.rem(shear + 1, shears)
    below = lax.rem(shear + shears - 1, shears)

    def put(at):
        for to, first, second in ((above, up0, up1), (below, down0, down1), (shear, up0, down0)):
            rows_ref[at * shears + to, 0:NZ, :] = first
            rows_ref[at * shears + to, NZ : 2 * NZ, :] = second
        for extra in range(2, shears - 1):
            rows_ref[at * shears + lax.rem(shear + extra, shears)] = jnp.zeros((2 * NZ, LANES), jnp.float32)

    if flows <= 8:
        for at in range(flows):
            put(at)
    else:
        pl.loop(0, flows)(put)

    for out, near, far, lanes in ((east_ref, width - 1, width - 2, EAST), (west_ref, 0, 1, WEST)):
        for at, first in ((far, 0), (near, 5)):
            f = [column(f_ref, q, at, width) for q in range(19)]
            wanted = list(range(19)) if at == near else lanes
            post = relax(*moments(f), f, wanted)
            for q in wanted:
                post[q] = roll_y(roll_z(post[q], VELOCITY[q][2]), VELOCITY[q][1])
            for i, q in enumerate(lanes):
                out[first + i] = post[q]
            if at == near:
                for i, s in enumerate(classes(post, "y")):
                    out[10 + i] = s


def local_kernel(width, f_ref, a_ref):
    def step(x):
        f = [column(f_ref, q, x, width) for q in range(19)]
        post = relax(*moments(f), f, range(19))
        for q in range(19):
            cx, cy, cz = VELOCITY[q]
            a_ref[q, x + 1 + cx] = roll_y(roll_z(post[q], cz), cy)

    pl.loop(0, width, unroll=2)(step)
    for q in range(19):
        cx = VELOCITY[q][0]
        zero = jnp.zeros((NZ, LANES), jnp.float32)
        for x in (0, 1, width, width + 1):
            if not 0 <= x - 1 - cx < width:
                a_ref[q, x] = zero


def finish_kernel(
    flows, shears, width, cells, weight, a_ref, rows_ref, west_ref, east_ref, out_hbm,
    out_ref, sem_out,
):
    flow = lax.axis_index("flow")
    shear = lax.axis_index("shear")
    lane = lane_iota()
    total_x = flows * width
    at_bottom = shear == 0
    at_top = shear == shears - 1
    above = lax.rem(shear + 1, shears)
    below = lax.rem(shear + shears - 1, shears)
    k1, k2 = cells[0], cells[1]
    frac = [weight[s].astype(jnp.float32) / WEIGHT_DENOM for s in range(2)]
    one, zero = jnp.float32(1.0), jnp.float32(0.0)

    def window(start, source, vreg, half):
        first = lax.rem(flow * width + start - BASE + 2 * total_x, total_x)
        block = lax.div(first, width)
        skip = (first - block * width) * GAP
        a, b, c = [
            rows_ref[lax.rem(block + k, flows) * shears + source, vreg * NZ : (vreg + 1) * NZ, :]
            for k in range(3)
        ]
        if half:
            a, c = roll_y(a, HALF), roll_y(c, HALF)
        else:
            b = roll_y(b, HALF)
        both = jnp.where(lane < HALF, a, b)
        return pltpu.roll(jnp.where(lane >= skip, both, c), lax.rem(LANES - skip, LANES), 1)

    def side(upward):
        lanes = UP if upward else DOWN
        others = DOWN if upward else UP
        active = at_bottom if upward else at_top
        source = below if upward else above

        def starts(k, low):
            return k if low else -k - 1

        def coefs(s, low):
            pair = (one - frac[s], frac[s]) if low else (frac[s], one - frac[s])
            return jnp.where(active, pair[0], one), jnp.where(active, pair[1], zero)

        def mixed(v, pair):
            return pair[0] * v + pair[1] * roll_y(v, -GAP)

        start1 = jnp.where(active, starts(k1, upward), 0)
        start2 = jnp.where(active, starts(k2, upward), 0)
        start3 = jnp.where(active, starts(k2, upward) + starts(k1, not upward), 0)
        near = [mixed(window(start1, source, 0, h), coefs(0, upward)) for h in range(2)]
        ghost1 = {q: (near[i // GAP], i % GAP) for i, q in enumerate(lanes)}
        packs = [None] + [window(start2, source, v, h) for v, h in ((0, 1), (1, 0), (1, 1))]
        pair3 = coefs(0, not upward)
        own = 1 if upward else 0
        back = [mixed(window(start3, shear, own, h), pair3) for h in range(2)]

        def plane(at, by):
            return roll_y(packs[at // GAP], by * GAP - at % GAP)

        f = {}
        for i, q in enumerate(lanes):
            f[q] = plane(11 + i, VELOCITY[q][0])
        for i, q in enumerate(others):
            f[q] = roll_y(back[i // GAP], VELOCITY[q][0] * GAP - i % GAP)
        mid, plus, minus = plane(5, 0), plane(6, 1), plane(7, -1)
        midz, plusz, minusz = plane(8, 0), plane(9, 1), plane(10, -1)
        up = [f[q] for q in UP]
        down = [f[q] for q in DOWN]
        sum_up = up[0] + up[1] + up[2] + up[3] + up[4]
        sum_down = down[0] + down[1] + down[2] + down[3] + down[4]
        rho = (mid + plus + minus) + (sum_up + sum_down)
        jx = (plus - minus) + ((f[7] - f[10]) + (f[9] - f[8]))
        jy = sum_up - sum_down
        jz = (midz + plusz + minusz) + ((f[15] - f[17]) + (f[18] - f[16]))
        post = relax(rho, jx, jy, jz, f, lanes)
        boost = jnp.where(active, -BOOST if upward else BOOST, 0.0).astype(jnp.float32)
        pair2 = coefs(1, upward)
        ghost2 = {}
        for q in lanes:
            cx, _, cz = VELOCITY[q]
            p = post[q] + cx * boost * rho if cx else post[q]
            ghost2[q] = (roll_z(mixed(p, pair2), cz), 0)
        return ghost1, ghost2

    up1, up2 = side(True)
    down1, down2 = side(False)
    ghosts1 = {**up1, **down1}
    ghosts2 = {**up2, **down2}
    at_first = lane == 0
    at_last = lane == LANES - 1

    def insert(v, ghosts, q, x):
        cy = VELOCITY[q][1]
        if cy == 0:
            return v
        g, slot = ghosts[q]
        by = (0 if cy > 0 else LANES - 1) - ((x + BASE) * GAP + slot)
        if isinstance(x, int):
            moved = roll_y(g, by)
        else:
            moved = pltpu.roll(g, lax.rem(by + LANES, LANES), 1)
        return jnp.where(at_first if cy > 0 else at_last, moved, v)

    def arrived(q, x):
        if isinstance(x, int) and x == 0 and q in EAST:
            return west_ref[5 + EAST.index(q)]
        if isinstance(x, int) and x == width - 1 and q in WEST:
            return east_ref[5 + WEST.index(q)]
        return a_ref[q, x + 1]

    def put(q, x, post):
        cx, cy, cz = VELOCITY[q]
        v = insert(roll_y(roll_z(post[q], cz), cy), ghosts2, q, x)
        out_ref[q, pl.ds(x + cx, NZ, stride=width), :] = v

    def inner(x, keep):
        f = [insert(arrived(q, x), ghosts1, q, x - VELOCITY[q][0]) for q in range(19)]
        wanted = [q for q in range(19) if VELOCITY[q][0] != -keep or keep == 0]
        post = relax(*moments(f), f, wanted)
        for q in wanted:
            put(q, x, post)

    for x, halo, entering, leaving in ((-1, west_ref, EAST, WEST), (width, east_ref, WEST, EAST)):
        cx = VELOCITY[entering[0]][0]
        f = {q: insert(halo[i], ghosts1, q, x - cx) for i, q in enumerate(entering)}
        for q in leaving:
            f[q] = insert(a_ref[q, x + 1], ghosts1, q, x + cx)

        def edge_value(q):
            g, slot = ghosts1[q]
            return roll_y(g, (0 if VELOCITY[q][1] > 0 else LANES - 1) - ((x + BASE) * GAP + slot))

        n, np_, nm = edge_value(3), edge_value(15), edge_value(17)
        s, sm, sp = edge_value(4), edge_value(16), edge_value(18)
        plus = jnp.where(at_first, n + np_ + nm, halo[11])
        minus = jnp.where(at_last, s + sm + sp, halo[12])
        plusz = jnp.where(at_first, np_ - nm, halo[14])
        minusz = jnp.where(at_last, sp - sm, halo[15])
        sum_e = f[1] + f[7] + f[9] + f[11] + f[13]
        sum_w = f[2] + f[8] + f[10] + f[12] + f[14]
        rho = (halo[10] + plus + minus) + (sum_e + sum_w)
        jx = sum_e - sum_w
        jy = (plus - minus) + ((f[7] - f[8]) + (f[10] - f[9]))
        jz = (halo[13] + plusz + minusz) + ((f[11] - f[12]) + (f[14] - f[13]))
        post = relax(rho, jx, jy, jz, f, entering)
        for q in entering:
            put(q, x, post)

    inner(0, 1)
    pl.loop(1, width - 1, unroll=7)(lambda x: inner(x, 0))
    inner(width - 1, -1)
    store = pltpu.make_async_copy(out_ref, out_hbm, sem_out)
    store.start()
    store.wait()


def per_device(populations, le_cells, le_weight):
    width = populations.shape[2]
    height = populations.shape[3]
    flows = lax.axis_size("flow")
    shears = lax.axis_size("shear")
    assert populations.shape[:2] == (19, NZ) and height == LANES
    assert width * GAP == HALF and shears >= 3 and flows >= 3
    f32 = jnp.float32
    f = populations.reshape(19, NZ * width, height)
    vmem = pl.BlockSpec(memory_space=pltpu.VMEM)
    anyspace = pl.BlockSpec(memory_space=pl.ANY)
    hbm = pl.BlockSpec(memory_space=pltpu.HBM)
    smem = pl.BlockSpec(memory_space=pltpu.SMEM)
    params = pltpu.CompilerParams(vmem_limit_bytes=32 * 1024 * 1024)
    devices = flows * shears

    def body(kernel, *fixed):
        return lambda *refs: kernel(*fixed, *refs)

    rows, east, west = pl.pallas_call(
        body(pack_kernel, flows, shears, width),
        out_shape=[
            jax.ShapeDtypeStruct((devices, 2 * NZ, LANES), f32),
            jax.ShapeDtypeStruct((16, NZ, LANES), f32),
            jax.ShapeDtypeStruct((16, NZ, LANES), f32),
        ],
        in_specs=[vmem],
        out_specs=[vmem] * 3,
        compiler_params=params,
        name="pack",
    )(f)
    rows = lax.all_to_all(rows, ("flow", "shear"), 0, 0, tiled=True)
    from_west = lax.ppermute(east, "flow", [(i, (i + 1) % flows) for i in range(flows)])
    from_east = lax.ppermute(west, "flow", [(i, (i - 1) % flows) for i in range(flows)])
    streamed = pl.pallas_call(
        body(local_kernel, width),
        out_shape=jax.ShapeDtypeStruct((19, width + 2, NZ, LANES), f32),
        in_specs=[vmem],
        out_specs=vmem,
        compiler_params=params,
        cost_estimate=pl.CostEstimate(flops=8_000_000, bytes_accessed=2_700_000, transcendentals=0),
        name="local",
    )(f)
    out = pl.pallas_call(
        body(finish_kernel, flows, shears, width),
        out_shape=jax.ShapeDtypeStruct((19, NZ * width, LANES), f32),
        in_specs=[smem, smem, vmem, vmem, vmem, vmem],
        out_specs=anyspace,
        scratch_shapes=[
            pltpu.VMEM((19, NZ * width, LANES), f32),
            pltpu.SemaphoreType.DMA,
        ],
        compiler_params=params,
        name="finish",
    )(le_cells, le_weight, streamed, rows, from_west, from_east)
    return out.reshape(populations.shape)


def solution(mesh):
    return jax.shard_map(
        per_device,
        mesh=mesh,
        in_specs=(P(None, None, "flow", "shear"), P(), P()),
        out_specs=P(None, None, "flow", "shear"),
        check_vma=False,
    )
```

```python
import jax
import jax.numpy as jnp
from jax import lax
from jax.experimental import pallas as pl
from jax.experimental.pallas import tpu as pltpu
from jax.sharding import PartitionSpec as P

WEIGHT_DENOM = 256
VELOCITY = [
    (0, 0, 0),
    (1, 0, 0),
    (-1, 0, 0),
    (0, 1, 0),
    (0, -1, 0),
    (0, 0, 1),
    (0, 0, -1),
    (1, 1, 0),
    (-1, -1, 0),
    (1, -1, 0),
    (-1, 1, 0),
    (1, 0, 1),
    (-1, 0, -1),
    (1, 0, -1),
    (-1, 0, 1),
    (0, 1, 1),
    (0, -1, -1),
    (0, 1, -1),
    (0, -1, 1),
]
WEIGHTS = [1.0 / 3.0] + [1.0 / 18.0] * 6 + [1.0 / 36.0] * 12
EAST = [1, 7, 9, 11, 13]
WEST = [2, 8, 10, 12, 14]
UP = [3, 7, 10, 15, 17]
DOWN = [4, 8, 9, 16, 18]
OMEGA = 1.0 / 0.6
WALL_SPEED = 0.1
BOOST = 3.0 * WALL_SPEED / 36.0
NZ = 8
LANES = 128
GAP = 4
HALF = 64
BASE = 2


def lane_iota():
    return lax.broadcasted_iota(jnp.int32, (NZ, LANES), 1)


def roll_y(v, by):
    by = by % LANES
    return pltpu.roll(v, by, 1) if by else v


def roll_z(v, by):
    by = by % NZ
    return pltpu.roll(v, by, 0) if by else v


def moments(f):
    e = f[1] + f[11] + f[13]
    w = f[2] + f[12] + f[14]
    n = f[3] + f[15] + f[17]
    s = f[4] + f[16] + f[18]
    d79 = f[7] + f[9]
    d810 = f[8] + f[10]
    rho = ((f[0] + f[5]) + f[6]) + (e + w) + (n + s) + (d79 + d810)
    jx = (e - w) + (d79 - d810)
    jy = (n - s) + ((f[7] - f[9]) + (f[10] - f[8]))
    jz = (f[5] - f[6]) + ((f[11] - f[12]) + (f[14] - f[13])) + ((f[15] - f[16]) + (f[18] - f[17]))
    return rho, jx, jy, jz


def relax(rho, jx, jy, jz, f, wanted):
    inv = 1.0 / rho
    ux, uy, uz = jx * inv, jy * inv, jz * inv
    base = (rho - 1.5 * (jx * ux + jy * uy + jz * uz)) * (OMEGA / 36.0)
    keep = 1.0 - OMEGA
    post = {}
    done = set()
    for q in wanted:
        if q in done:
            continue
        cx, cy, cz = VELOCITY[q]
        if q == 0:
            post[0] = keep * f[0] + 12.0 * base
            continue
        opposite = VELOCITY.index((-cx, -cy, -cz))
        jc, uc = None, None
        for c, j, u in ((cx, jx, ux), (cy, jy, uy), (cz, jz, uz)):
            if c:
                if jc is None:
                    jc, uc = (j, u) if c > 0 else (-j, -u)
                else:
                    jc, uc = (jc + j, uc + u) if c > 0 else (jc - j, uc - u)
        scale = WEIGHTS[q] * 36.0
        even = base * scale if scale != 1.0 else base
        even = even + (jc * uc) * (4.5 * OMEGA * WEIGHTS[q])
        odd = jc * (3.0 * OMEGA * WEIGHTS[q])
        post[q] = keep * f[q] + (even + odd)
        done.add(q)
        if opposite in wanted:
            post[opposite] = keep * f[opposite] + (even - odd)
            done.add(opposite)
    return post


def classes(p, across):
    if across == "x":
        plus, minus = (1, 11, 13), (2, 12, 14)
    else:
        plus, minus = (3, 15, 17), (4, 16, 18)
    rising, falling = plus[1], plus[2]
    low, high = minus[1], minus[2]
    return [
        p[0] + p[5] + p[6],
        p[plus[0]] + p[rising] + p[falling],
        p[minus[0]] + p[low] + p[high],
        p[5] - p[6],
        p[rising] - p[falling],
        p[high] - p[low],
    ]


def column(ref, q, x, width):
    return ref[q, pl.ds(x, NZ, stride=width), :]


def pack_kernel(flows, shears, width, f_ref, rows_ref, near_ref, far_ref):
    shear = lax.axis_index("shear")
    lane = lane_iota()
    boost_up = jnp.where(shear == shears - 1, -BOOST, 0.0).astype(jnp.float32)
    boost_down = jnp.where(shear == 0, BOOST, 0.0).astype(jnp.float32)
    here = [(lane >= x * GAP) & (lane < (x + 1) * GAP) for x in range(width)]
    edge = []
    for q in range(19):
        total = jnp.ones((NZ, LANES), jnp.float32)
        for x in range(width):
            total = jnp.where(here[x], roll_y(column(f_ref, q, x, width), x * GAP + 2), total)
        edge.append(total)
    rho, jx, jy, jz = moments(edge)
    post = relax(rho, jx, jy, jz, edge, range(19))
    post = {q: roll_z(post[q], VELOCITY[q][2]) for q in range(19)}
    sums = classes(post, "x")

    def groups(ghosts, outer, at, far):
        planes = [(g, at) for g in ghosts] + [(s, at) for s in sums] + [(o, far) for o in outer]
        vregs = []
        for v in range(2):
            total = None
            for half in range(2):
                for slot in range(GAP):
                    plane, row = planes[(v * 2 + half) * GAP + slot]
                    moved = roll_y(plane, half * HALF + slot - row)
                    if total is None:
                        total = moved
                    else:
                        inside = (lane >= half * HALF) & (lane < (half + 1) * HALF)
                        total = jnp.where(inside & (lane % GAP == slot), moved, total)
            vregs.append(total)
        return vregs

    ups = [post[q] + VELOCITY[q][0] * boost_up * rho if VELOCITY[q][0] else post[q] for q in UP]
    downs = [post[q] + VELOCITY[q][0] * boost_down * rho if VELOCITY[q][0] else post[q] for q in DOWN]
    up0, up1 = groups(ups, [post[q] for q in UP], 1, 0)
    down0, down1 = groups(downs, [post[q] for q in DOWN], 2, 3)
    above = lax.rem(shear + 1, shears)
    below = lax.rem(shear + shears - 1, shears)

    def put(at):
        for to, first, second in ((above, up0, up1), (below, down0, down1), (shear, up0, down0)):
            rows_ref[at * shears + to, 0:NZ, :] = first
            rows_ref[at * shears + to, NZ : 2 * NZ, :] = second
        for extra in range(2, shears - 1):
            rows_ref[at * shears + lax.rem(shear + extra, shears)] = jnp.zeros((2 * NZ, LANES), jnp.float32)

    if flows <= 8:
        for at in range(flows):
            put(at)
    else:
        pl.loop(0, flows)(put)

    packs = []
    for near, far, lanes in ((width - 1, width - 2, EAST), (0, 1, WEST)):
        planes = []
        for at in (far, near):
            f = [column(f_ref, q, at, width) for q in range(19)]
            wanted = list(range(19)) if at == near else lanes
            post = relax(*moments(f), f, wanted)
            for q in wanted:
                post[q] = roll_y(roll_z(post[q], VELOCITY[q][2]), VELOCITY[q][1])
            planes += [post[q] for q in lanes]
        still, plus, minus, still_z, plus_z, minus_z = classes(post, "y")
        plus, plus_z = [jnp.where(lane == 0, 0.0, v) for v in (plus, plus_z)]
        minus, minus_z = [jnp.where(lane == LANES - 1, 0.0, v) for v in (minus, minus_z)]
        packs.append(planes + [still + (plus + minus), plus - minus, still_z + (plus_z + minus_z)])
    even = lax.rem(lax.axis_index("flow"), 2) == 0
    for i, (to_east, to_west) in enumerate(zip(*packs)):
        near_ref[i] = jnp.where(even, to_east, to_west)
        far_ref[i] = jnp.where(even, to_west, to_east)


def local_kernel(width, f_ref, a_ref):
    def step(x):
        f = [column(f_ref, q, x, width) for q in range(19)]
        post = relax(*moments(f), f, range(19))
        for q in range(19):
            cx, cy, cz = VELOCITY[q]
            a_ref[q, x + 1 + cx] = roll_y(roll_z(post[q], cz), cy)

    pl.loop(0, width, unroll=2)(step)
    for q in range(19):
        cx = VELOCITY[q][0]
        zero = jnp.zeros((NZ, LANES), jnp.float32)
        for x in (0, 1, width, width + 1):
            if not 0 <= x - 1 - cx < width:
                a_ref[q, x] = zero


def finish_kernel(
    flows, shears, width, cells, weight, a_ref, rows_ref, far_ref, near_ref, out_hbm,
    out_ref, sem_out,
):
    flow = lax.axis_index("flow")
    shear = lax.axis_index("shear")
    lane = lane_iota()
    total_x = flows * width
    even = lax.rem(flow, 2) == 0
    at_bottom = shear == 0
    at_top = shear == shears - 1
    above = lax.rem(shear + 1, shears)
    below = lax.rem(shear + shears - 1, shears)
    k1, k2 = cells[0], cells[1]
    frac = [weight[s].astype(jnp.float32) / WEIGHT_DENOM for s in range(2)]
    one, zero = jnp.float32(1.0), jnp.float32(0.0)

    def window(start, source, vreg, half):
        first = lax.rem(flow * width + start - BASE + 2 * total_x, total_x)
        block = lax.div(first, width)
        skip = (first - block * width) * GAP
        a, b, c = [
            rows_ref[lax.rem(block + k, flows) * shears + source, vreg * NZ : (vreg + 1) * NZ, :]
            for k in range(3)
        ]
        if half:
            a, c = roll_y(a, HALF), roll_y(c, HALF)
        else:
            b = roll_y(b, HALF)
        both = jnp.where(lane < HALF, a, b)
        return pltpu.roll(jnp.where(lane >= skip, both, c), lax.rem(LANES - skip, LANES), 1)

    def side(upward):
        lanes = UP if upward else DOWN
        others = DOWN if upward else UP
        active = at_bottom if upward else at_top
        source = below if upward else above

        def starts(k, low):
            return k if low else -k - 1

        def coefs(s, low):
            pair = (one - frac[s], frac[s]) if low else (frac[s], one - frac[s])
            return jnp.where(active, pair[0], one), jnp.where(active, pair[1], zero)

        def mixed(v, pair):
            return pair[0] * v + pair[1] * roll_y(v, -GAP)

        start1 = jnp.where(active, starts(k1, upward), 0)
        start2 = jnp.where(active, starts(k2, upward), 0)
        start3 = jnp.where(active, starts(k2, upward) + starts(k1, not upward), 0)
        near = [mixed(window(start1, source, 0, h), coefs(0, upward)) for h in range(2)]
        ghost1 = {q: (near[i // GAP], i % GAP) for i, q in enumerate(lanes)}
        packs = [None] + [window(start2, source, v, h) for v, h in ((0, 1), (1, 0), (1, 1))]
        pair3 = coefs(0, not upward)
        own = 1 if upward else 0
        back = [mixed(window(start3, shear, own, h), pair3) for h in range(2)]

        def plane(at, by):
            return roll_y(packs[at // GAP], by * GAP - at % GAP)

        f = {}
        for i, q in enumerate(lanes):
            f[q] = plane(11 + i, VELOCITY[q][0])
        for i, q in enumerate(others):
            f[q] = roll_y(back[i // GAP], VELOCITY[q][0] * GAP - i % GAP)
        mid, plus, minus = plane(5, 0), plane(6, 1), plane(7, -1)
        midz, plusz, minusz = plane(8, 0), plane(9, 1), plane(10, -1)
        up = [f[q] for q in UP]
        down = [f[q] for q in DOWN]
        sum_up = up[0] + up[1] + up[2] + up[3] + up[4]
        sum_down = down[0] + down[1] + down[2] + down[3] + down[4]
        rho = (mid + plus + minus) + (sum_up + sum_down)
        jx = (plus - minus) + ((f[7] - f[10]) + (f[9] - f[8]))
        jy = sum_up - sum_down
        jz = (midz + plusz + minusz) + ((f[15] - f[17]) + (f[18] - f[16]))
        post = relax(rho, jx, jy, jz, f, lanes)
        boost = jnp.where(active, -BOOST if upward else BOOST, 0.0).astype(jnp.float32)
        pair2 = coefs(1, upward)
        ghost2 = {}
        for q in lanes:
            cx, _, cz = VELOCITY[q]
            p = post[q] + cx * boost * rho if cx else post[q]
            ghost2[q] = (roll_z(mixed(p, pair2), cz), 0)
        return ghost1, ghost2

    up1, up2 = side(True)
    down1, down2 = side(False)
    at_first = lane == 0
    at_last = lane == LANES - 1
    odd = lane % GAP == 1

    def pairs(ups, downs, streamed):
        found = []
        for u, d in zip(UP, DOWN):
            (gu, su), (gd, sd) = ups[u], downs[d]
            along = [VELOCITY[q][0] * GAP if streamed else 0 for q in (u, d)]
            found.append(jnp.where(odd, roll_y(gu, along[0] + 1 - su), roll_y(gd, along[1] - sd)))
        return found

    pairs1 = pairs(up1, down1, True)
    pairs2 = pairs(up2, down2, False)

    def beyond(found, x):
        return [roll_y(v, -1 - (x + BASE) * GAP) for v in found]

    def insert(v, q, edge):
        if q in UP:
            return jnp.where(at_first, edge[UP.index(q)], v)
        if q in DOWN:
            return jnp.where(at_last, edge[DOWN.index(q)], v)
        return v

    def from_west(i):
        return jnp.where(even, far_ref[i], near_ref[i])

    def from_east(i):
        return jnp.where(even, near_ref[i], far_ref[i])

    def arrived(q, x):
        if x == 0 and q in EAST:
            return from_west(5 + EAST.index(q))
        if x == width - 1 and q in WEST:
            return from_east(5 + WEST.index(q))
        return a_ref[q, x + 1]

    def put(post, x):
        edge = beyond(pairs2, x)
        for q in post:
            cx, cy, cz = VELOCITY[q]
            if 0 <= x + cx < width:
                v = insert(roll_y(roll_z(post[q], cz), cy), q, edge)
                out_ref[q, pl.ds(x + cx, NZ, stride=width), :] = v

    for x, halo, entering, leaving in ((-1, from_west, EAST, WEST), (width, from_east, WEST, EAST)):
        edge = beyond(pairs1, x)
        f = {q: insert(halo(i), q, edge) for i, q in enumerate(entering)}
        for q in leaving:
            f[q] = insert(a_ref[q, x + 1], q, edge)
        level, rising, falling = edge[0] + edge[3] + edge[4], edge[3], edge[4]
        more = jnp.where(at_first | at_last, level, 0.0)
        more_y = jnp.where(at_first, level, jnp.where(at_last, -level, 0.0))
        turn = rising - falling
        more_z = jnp.where(at_first, turn, jnp.where(at_last, -turn, 0.0))
        sum_e = f[1] + f[7] + f[9] + f[11] + f[13]
        sum_w = f[2] + f[8] + f[10] + f[12] + f[14]
        rho = (halo(10) + more) + (sum_e + sum_w)
        jx = sum_e - sum_w
        jy = (halo(11) + more_y) + ((f[7] - f[8]) + (f[10] - f[9]))
        jz = (halo(12) + more_z) + ((f[11] - f[12]) + (f[14] - f[13]))
        put(relax(rho, jx, jy, jz, f, entering), x)

    for x in range(width):
        edge = beyond(pairs1, x)
        f = [insert(arrived(q, x), q, edge) for q in range(19)]
        post = relax(*moments(f), f, range(19))
        put(post, x)

    store = pltpu.make_async_copy(out_ref, out_hbm, sem_out)
    store.start()
    store.wait()


def per_device(populations, le_cells, le_weight):
    width = populations.shape[2]
    height = populations.shape[3]
    flows = lax.axis_size("flow")
    shears = lax.axis_size("shear")
    assert populations.shape[:2] == (19, NZ) and height == LANES
    assert width * GAP == HALF and shears >= 3 and flows >= 4 and flows % 2 == 0
    f32 = jnp.float32
    f = populations.reshape(19, NZ * width, height)
    vmem = pl.BlockSpec(memory_space=pltpu.VMEM)
    anyspace = pl.BlockSpec(memory_space=pl.ANY)
    hbm = pl.BlockSpec(memory_space=pltpu.HBM)
    smem = pl.BlockSpec(memory_space=pltpu.SMEM)
    params = pltpu.CompilerParams(vmem_limit_bytes=32 * 1024 * 1024)
    devices = flows * shears

    def body(kernel, *fixed):
        return lambda *refs: kernel(*fixed, *refs)

    rows, near, far = pl.pallas_call(
        body(pack_kernel, flows, shears, width),
        out_shape=[
            jax.ShapeDtypeStruct((devices, 2 * NZ, LANES), f32),
            jax.ShapeDtypeStruct((13, NZ, LANES), f32),
            jax.ShapeDtypeStruct((13, NZ, LANES), f32),
        ],
        in_specs=[vmem],
        out_specs=[vmem] * 3,
        compiler_params=params,
        name="pack",
    )(f)
    rows = lax.all_to_all(rows, ("flow", "shear"), 0, 0, tiled=True)
    from_far = lax.ppermute(far, "flow", [(i, (i - 1 + i % 2 * 2) % flows) for i in range(flows)])
    from_near = lax.ppermute(near, "flow", [(i, i + 1 - i % 2 * 2) for i in range(flows)])
    streamed = pl.pallas_call(
        body(local_kernel, width),
        out_shape=jax.ShapeDtypeStruct((19, width + 2, NZ, LANES), f32),
        in_specs=[vmem],
        out_specs=vmem,
        compiler_params=params,
        cost_estimate=pl.CostEstimate(flops=8_000_000, bytes_accessed=2_700_000, transcendentals=0),
        name="local",
    )(f)
    out = pl.pallas_call(
        body(finish_kernel, flows, shears, width),
        out_shape=jax.ShapeDtypeStruct((19, NZ * width, LANES), f32),
        in_specs=[smem, smem, vmem, vmem, vmem, vmem],
        out_specs=anyspace,
        scratch_shapes=[
            pltpu.VMEM((19, NZ * width, LANES), f32),
            pltpu.SemaphoreType.DMA,
        ],
        compiler_params=params,
        name="finish",
    )(le_cells, le_weight, streamed, rows, from_far, from_near)
    return out.reshape(populations.shape)


def solution(mesh):
    return jax.shard_map(
        per_device,
        mesh=mesh,
        in_specs=(P(None, None, "flow", "shear"), P(), P()),
        out_specs=P(None, None, "flow", "shear"),
        check_vma=False,
    )
```

```python
import jax
import jax.numpy as jnp
from jax import lax
from jax.experimental import pallas as pl
from jax.experimental.pallas import tpu as pltpu
from jax.sharding import PartitionSpec as P

WEIGHT_DENOM = 256
VELOCITY = [
    (0, 0, 0),
    (1, 0, 0),
    (-1, 0, 0),
    (0, 1, 0),
    (0, -1, 0),
    (0, 0, 1),
    (0, 0, -1),
    (1, 1, 0),
    (-1, -1, 0),
    (1, -1, 0),
    (-1, 1, 0),
    (1, 0, 1),
    (-1, 0, -1),
    (1, 0, -1),
    (-1, 0, 1),
    (0, 1, 1),
    (0, -1, -1),
    (0, 1, -1),
    (0, -1, 1),
]
WEIGHTS = [1.0 / 3.0] + [1.0 / 18.0] * 6 + [1.0 / 36.0] * 12
EAST = [1, 7, 9, 11, 13]
WEST = [2, 8, 10, 12, 14]
UP = [3, 7, 10, 15, 17]
DOWN = [4, 8, 9, 16, 18]
OMEGA = 1.0 / 0.6
WALL_SPEED = 0.1
BOOST = 3.0 * WALL_SPEED / 36.0
NZ = 8
LANES = 128
GAP = 4
HALF = 64
BASE = 2


def lane_iota():
    return lax.broadcasted_iota(jnp.int32, (NZ, LANES), 1)


def roll_y(v, by):
    by = by % LANES
    return pltpu.roll(v, by, 1) if by else v


def roll_z(v, by):
    by = by % NZ
    return pltpu.roll(v, by, 0) if by else v


def moments(f):
    e = f[1] + f[11] + f[13]
    w = f[2] + f[12] + f[14]
    n = f[3] + f[15] + f[17]
    s = f[4] + f[16] + f[18]
    d79 = f[7] + f[9]
    d810 = f[8] + f[10]
    rho = ((f[0] + f[5]) + f[6]) + (e + w) + (n + s) + (d79 + d810)
    jx = (e - w) + (d79 - d810)
    jy = (n - s) + ((f[7] - f[9]) + (f[10] - f[8]))
    jz = (f[5] - f[6]) + ((f[11] - f[12]) + (f[14] - f[13])) + ((f[15] - f[16]) + (f[18] - f[17]))
    return rho, jx, jy, jz


def relax(rho, jx, jy, jz, f, wanted):
    inv = 1.0 / rho
    ux, uy, uz = jx * inv, jy * inv, jz * inv
    base = (rho - 1.5 * (jx * ux + jy * uy + jz * uz)) * (OMEGA / 36.0)
    keep = 1.0 - OMEGA
    post = {}
    done = set()
    for q in wanted:
        if q in done:
            continue
        cx, cy, cz = VELOCITY[q]
        if q == 0:
            post[0] = keep * f[0] + 12.0 * base
            continue
        opposite = VELOCITY.index((-cx, -cy, -cz))
        jc, uc = None, None
        for c, j, u in ((cx, jx, ux), (cy, jy, uy), (cz, jz, uz)):
            if c:
                if jc is None:
                    jc, uc = (j, u) if c > 0 else (-j, -u)
                else:
                    jc, uc = (jc + j, uc + u) if c > 0 else (jc - j, uc - u)
        scale = WEIGHTS[q] * 36.0
        even = base * scale if scale != 1.0 else base
        even = even + (jc * uc) * (4.5 * OMEGA * WEIGHTS[q])
        odd = jc * (3.0 * OMEGA * WEIGHTS[q])
        post[q] = keep * f[q] + (even + odd)
        done.add(q)
        if opposite in wanted:
            post[opposite] = keep * f[opposite] + (even - odd)
            done.add(opposite)
    return post


def classes(p, across):
    if across == "x":
        plus, minus = (1, 11, 13), (2, 12, 14)
    else:
        plus, minus = (3, 15, 17), (4, 16, 18)
    rising, falling = plus[1], plus[2]
    low, high = minus[1], minus[2]
    return [
        p[0] + p[5] + p[6],
        p[plus[0]] + p[rising] + p[falling],
        p[minus[0]] + p[low] + p[high],
        p[5] - p[6],
        p[rising] - p[falling],
        p[high] - p[low],
    ]


def column(ref, q, x, width):
    return ref[q, pl.ds(x, NZ, stride=width), :]


def pack_kernel(flows, shears, width, f_ref, rows_ref, near_ref, far_ref):
    shear = lax.axis_index("shear")
    lane = lane_iota()
    boost_up = jnp.where(shear == shears - 1, -BOOST, 0.0).astype(jnp.float32)
    boost_down = jnp.where(shear == 0, BOOST, 0.0).astype(jnp.float32)
    here = [(lane >= x * GAP) & (lane < (x + 1) * GAP) for x in range(width)]
    edge = []
    for q in range(19):
        total = jnp.ones((NZ, LANES), jnp.float32)
        for x in range(width):
            total = jnp.where(here[x], roll_y(column(f_ref, q, x, width), x * GAP + 2), total)
        edge.append(total)
    rho, jx, jy, jz = moments(edge)
    post = relax(rho, jx, jy, jz, edge, range(19))
    post = {q: roll_z(post[q], VELOCITY[q][2]) for q in range(19)}
    sums = classes(post, "x")

    def groups(ghosts, outer, at, far):
        planes = [(g, at) for g in ghosts] + [(s, at) for s in sums] + [(o, far) for o in outer]
        vregs = []
        for v in range(2):
            total = None
            for half in range(2):
                for slot in range(GAP):
                    plane, row = planes[(v * 2 + half) * GAP + slot]
                    moved = roll_y(plane, half * HALF + slot - row)
                    if total is None:
                        total = moved
                    else:
                        inside = (lane >= half * HALF) & (lane < (half + 1) * HALF)
                        total = jnp.where(inside & (lane % GAP == slot), moved, total)
            vregs.append(total)
        return vregs

    ups = [post[q] + VELOCITY[q][0] * boost_up * rho if VELOCITY[q][0] else post[q] for q in UP]
    downs = [post[q] + VELOCITY[q][0] * boost_down * rho if VELOCITY[q][0] else post[q] for q in DOWN]
    up0, up1 = groups(ups, [post[q] for q in UP], 1, 0)
    down0, down1 = groups(downs, [post[q] for q in DOWN], 2, 3)
    above = lax.rem(shear + 1, shears)
    below = lax.rem(shear + shears - 1, shears)

    def put(at):
        for to, first, second in ((above, up0, up1), (below, down0, down1), (shear, up0, down0)):
            rows_ref[at * shears + to, 0:NZ, :] = first
            rows_ref[at * shears + to, NZ : 2 * NZ, :] = second
        for extra in range(2, shears - 1):
            rows_ref[at * shears + lax.rem(shear + extra, shears)] = jnp.zeros((2 * NZ, LANES), jnp.float32)

    if flows <= 8:
        for at in range(flows):
            put(at)
    else:
        pl.loop(0, flows)(put)

    packs = []
    for near, far, lanes in ((width - 1, width - 2, EAST), (0, 1, WEST)):
        planes = []
        for at in (far, near):
            f = [column(f_ref, q, at, width) for q in range(19)]
            wanted = list(range(19)) if at == near else lanes
            post = relax(*moments(f), f, wanted)
            for q in wanted:
                post[q] = roll_y(roll_z(post[q], VELOCITY[q][2]), VELOCITY[q][1])
            planes += [post[q] for q in lanes]
        still, plus, minus, still_z, plus_z, minus_z = classes(post, "y")
        plus, plus_z = [jnp.where(lane == 0, 0.0, v) for v in (plus, plus_z)]
        minus, minus_z = [jnp.where(lane == LANES - 1, 0.0, v) for v in (minus, minus_z)]
        packs.append(planes + [still + (plus + minus), plus - minus, still_z + (plus_z + minus_z)])
    even = lax.rem(lax.axis_index("flow"), 2) == 0
    for i, (to_east, to_west) in enumerate(zip(*packs)):
        near_ref[i] = jnp.where(even, to_east, to_west)
        far_ref[i] = jnp.where(even, to_west, to_east)


def local_kernel(width, f_ref, a_ref):
    def step(x):
        f = [column(f_ref, q, x, width) for q in range(19)]
        post = relax(*moments(f), f, range(19))
        for q in range(19):
            cx, cy, cz = VELOCITY[q]
            a_ref[q, x + 1 + cx] = roll_y(roll_z(post[q], cz), cy)

    pl.loop(0, width, unroll=2)(step)
    for q in range(19):
        cx = VELOCITY[q][0]
        zero = jnp.zeros((NZ, LANES), jnp.float32)
        for x in (0, 1, width, width + 1):
            if not 0 <= x - 1 - cx < width:
                a_ref[q, x] = zero


def finish_kernel(
    flows, shears, width, cells, weight, a_ref, rows_ref, far_ref, near_ref, out_hbm,
    out_ref, sem_out,
):
    flow = lax.axis_index("flow")
    shear = lax.axis_index("shear")
    lane = lane_iota()
    total_x = flows * width
    even = lax.rem(flow, 2) == 0
    at_bottom = shear == 0
    at_top = shear == shears - 1
    above = lax.rem(shear + 1, shears)
    below = lax.rem(shear + shears - 1, shears)
    k1, k2 = cells[0], cells[1]
    frac = [weight[s].astype(jnp.float32) / WEIGHT_DENOM for s in range(2)]
    one, zero = jnp.float32(1.0), jnp.float32(0.0)

    def window(start, source, vreg, half):
        first = lax.rem(flow * width + start - BASE + 2 * total_x, total_x)
        block = lax.div(first, width)
        skip = (first - block * width) * GAP
        a, b, c = [
            rows_ref[lax.rem(block + k, flows) * shears + source, vreg * NZ : (vreg + 1) * NZ, :]
            for k in range(3)
        ]
        if half:
            a, c = roll_y(a, HALF), roll_y(c, HALF)
        else:
            b = roll_y(b, HALF)
        both = jnp.where(lane < HALF, a, b)
        return pltpu.roll(jnp.where(lane >= skip, both, c), lax.rem(LANES - skip, LANES), 1)

    def side(upward):
        lanes = UP if upward else DOWN
        others = DOWN if upward else UP
        active = at_bottom if upward else at_top
        source = below if upward else above

        def starts(k, low):
            return k if low else -k - 1

        def coefs(s, low):
            pair = (one - frac[s], frac[s]) if low else (frac[s], one - frac[s])
            return jnp.where(active, pair[0], one), jnp.where(active, pair[1], zero)

        def mixed(v, pair):
            return pair[0] * v + pair[1] * roll_y(v, -GAP)

        start1 = jnp.where(active, starts(k1, upward), 0)
        start2 = jnp.where(active, starts(k2, upward), 0)
        start3 = jnp.where(active, starts(k2, upward) + starts(k1, not upward), 0)
        near = [mixed(window(start1, source, 0, h), coefs(0, upward)) for h in range(2)]
        ghost1 = {q: (near[i // GAP], i % GAP) for i, q in enumerate(lanes)}
        packs = [None] + [window(start2, source, v, h) for v, h in ((0, 1), (1, 0), (1, 1))]
        pair3 = coefs(0, not upward)
        own = 1 if upward else 0
        back = [mixed(window(start3, shear, own, h), pair3) for h in range(2)]

        def plane(at, by):
            return roll_y(packs[at // GAP], by * GAP - at % GAP)

        f = {}
        for i, q in enumerate(lanes):
            f[q] = plane(11 + i, VELOCITY[q][0])
        for i, q in enumerate(others):
            f[q] = roll_y(back[i // GAP], VELOCITY[q][0] * GAP - i % GAP)
        mid, plus, minus = plane(5, 0), plane(6, 1), plane(7, -1)
        midz, plusz, minusz = plane(8, 0), plane(9, 1), plane(10, -1)
        up = [f[q] for q in UP]
        down = [f[q] for q in DOWN]
        sum_up = up[0] + up[1] + up[2] + up[3] + up[4]
        sum_down = down[0] + down[1] + down[2] + down[3] + down[4]
        rho = (mid + plus + minus) + (sum_up + sum_down)
        jx = (plus - minus) + ((f[7] - f[10]) + (f[9] - f[8]))
        jy = sum_up - sum_down
        jz = (midz + plusz + minusz) + ((f[15] - f[17]) + (f[18] - f[16]))
        post = relax(rho, jx, jy, jz, f, lanes)
        boost = jnp.where(active, -BOOST if upward else BOOST, 0.0).astype(jnp.float32)
        pair2 = coefs(1, upward)
        ghost2 = {}
        for q in lanes:
            cx, _, cz = VELOCITY[q]
            p = post[q] + cx * boost * rho if cx else post[q]
            ghost2[q] = (roll_z(mixed(p, pair2), cz), 0)
        return ghost1, ghost2

    up1, up2 = side(True)
    down1, down2 = side(False)
    at_first = lane == 0
    at_last = lane == LANES - 1
    odd = lane % GAP == 1

    def pairs(ups, downs, streamed):
        found = []
        for u, d in zip(UP, DOWN):
            (gu, su), (gd, sd) = ups[u], downs[d]
            along = [VELOCITY[q][0] * GAP if streamed else 0 for q in (u, d)]
            found.append(jnp.where(odd, roll_y(gu, along[0] + 1 - su), roll_y(gd, along[1] - sd)))
        return found

    pairs1 = pairs(up1, down1, True)
    pairs2 = pairs(up2, down2, False)

    def beyond(found, x):
        return [roll_y(v, -1 - (x + BASE) * GAP) for v in found]

    def insert(v, q, edge):
        if q in UP:
            return jnp.where(at_first, edge[UP.index(q)], v)
        if q in DOWN:
            return jnp.where(at_last, edge[DOWN.index(q)], v)
        return v

    def from_west(i):
        return jnp.where(even, far_ref[i], near_ref[i])

    def from_east(i):
        return jnp.where(even, near_ref[i], far_ref[i])

    def arrived(q, x):
        if x == 0 and q in EAST:
            return from_west(5 + EAST.index(q))
        if x == width - 1 and q in WEST:
            return from_east(5 + WEST.index(q))
        return a_ref[q, x + 1]

    def put(post, x):
        edge = beyond(pairs2, x)
        for q in post:
            cx, cy, cz = VELOCITY[q]
            if 0 <= x + cx < width:
                v = insert(roll_y(roll_z(post[q], cz), cy), q, edge)
                out_ref[q, pl.ds(x + cx, NZ, stride=width), :] = v

    for x, halo, entering, leaving in ((-1, from_west, EAST, WEST), (width, from_east, WEST, EAST)):
        edge = beyond(pairs1, x)
        f = {q: insert(halo(i), q, edge) for i, q in enumerate(entering)}
        for q in leaving:
            f[q] = insert(a_ref[q, x + 1], q, edge)
        level, rising, falling = edge[0] + edge[3] + edge[4], edge[3], edge[4]
        more = jnp.where(at_first | at_last, level, 0.0)
        more_y = jnp.where(at_first, level, jnp.where(at_last, -level, 0.0))
        turn = rising - falling
        more_z = jnp.where(at_first, turn, jnp.where(at_last, -turn, 0.0))
        sum_e = f[1] + f[7] + f[9] + f[11] + f[13]
        sum_w = f[2] + f[8] + f[10] + f[12] + f[14]
        rho = (halo(10) + more) + (sum_e + sum_w)
        jx = sum_e - sum_w
        jy = (halo(11) + more_y) + ((f[7] - f[8]) + (f[10] - f[9]))
        jz = (halo(12) + more_z) + ((f[11] - f[12]) + (f[14] - f[13]))
        put(relax(rho, jx, jy, jz, f, entering), x)

    rows_of = (19, NZ, width, LANES)
    half = width // 2
    stores = [
        pltpu.make_async_copy(
            out_ref.reshape(rows_of).at[:, :, a : a + half], out_hbm.reshape(rows_of).at[:, :, a : a + half], sem_out.at[i]
        )
        for i, a in enumerate((0, half))
    ]
    for x in range(width):
        edge = beyond(pairs1, x)
        f = [insert(arrived(q, x), q, edge) for q in range(19)]
        post = relax(*moments(f), f, range(19))
        put(post, x)
        if x == half:
            stores[0].start()
    stores[1].start()
    for store in stores:
        store.wait()


def per_device(populations, le_cells, le_weight):
    width = populations.shape[2]
    height = populations.shape[3]
    flows = lax.axis_size("flow")
    shears = lax.axis_size("shear")
    assert populations.shape[:2] == (19, NZ) and height == LANES
    assert width * GAP == HALF and shears >= 3 and flows >= 4 and flows % 2 == 0
    f32 = jnp.float32
    f = populations.reshape(19, NZ * width, height)
    vmem = pl.BlockSpec(memory_space=pltpu.VMEM)
    anyspace = pl.BlockSpec(memory_space=pl.ANY)
    hbm = pl.BlockSpec(memory_space=pltpu.HBM)
    smem = pl.BlockSpec(memory_space=pltpu.SMEM)
    params = pltpu.CompilerParams(vmem_limit_bytes=32 * 1024 * 1024)
    devices = flows * shears

    def body(kernel, *fixed):
        return lambda *refs: kernel(*fixed, *refs)

    rows, near, far = pl.pallas_call(
        body(pack_kernel, flows, shears, width),
        out_shape=[
            jax.ShapeDtypeStruct((devices, 2 * NZ, LANES), f32),
            jax.ShapeDtypeStruct((13, NZ, LANES), f32),
            jax.ShapeDtypeStruct((13, NZ, LANES), f32),
        ],
        in_specs=[vmem],
        out_specs=[vmem] * 3,
        compiler_params=params,
        name="pack",
    )(f)
    rows = lax.all_to_all(rows, ("flow", "shear"), 0, 0, tiled=True)
    from_far = lax.ppermute(far, "flow", [(i, (i - 1 + i % 2 * 2) % flows) for i in range(flows)])
    from_near = lax.ppermute(near, "flow", [(i, i + 1 - i % 2 * 2) for i in range(flows)])
    streamed = pl.pallas_call(
        body(local_kernel, width),
        out_shape=jax.ShapeDtypeStruct((19, width + 2, NZ, LANES), f32),
        in_specs=[vmem],
        out_specs=vmem,
        compiler_params=params,
        cost_estimate=pl.CostEstimate(flops=8_000_000, bytes_accessed=2_700_000, transcendentals=0),
        name="local",
    )(f)
    out = pl.pallas_call(
        body(finish_kernel, flows, shears, width),
        out_shape=jax.ShapeDtypeStruct((19, NZ * width, LANES), f32),
        in_specs=[vmem, vmem, vmem, vmem, vmem, vmem],
        out_specs=anyspace,
        scratch_shapes=[
            pltpu.VMEM((19, NZ * width, LANES), f32),
            pltpu.SemaphoreType.DMA((2,)),
        ],
        compiler_params=params,
        name="finish",
    )(le_cells, le_weight, streamed, rows, from_far, from_near)
    return out.reshape(populations.shape)


def solution(mesh):
    return jax.shard_map(
        per_device,
        mesh=mesh,
        in_specs=(P(None, None, "flow", "shear"), P(), P()),
        out_specs=P(None, None, "flow", "shear"),
        check_vma=False,
    )
```

```python
import jax
import jax.numpy as jnp
from jax import lax
from jax.experimental import pallas as pl
from jax.experimental.pallas import tpu as pltpu
from jax.sharding import PartitionSpec as P

WEIGHT_DENOM = 256
VELOCITY = [
    (0, 0, 0),
    (1, 0, 0),
    (-1, 0, 0),
    (0, 1, 0),
    (0, -1, 0),
    (0, 0, 1),
    (0, 0, -1),
    (1, 1, 0),
    (-1, -1, 0),
    (1, -1, 0),
    (-1, 1, 0),
    (1, 0, 1),
    (-1, 0, -1),
    (1, 0, -1),
    (-1, 0, 1),
    (0, 1, 1),
    (0, -1, -1),
    (0, 1, -1),
    (0, -1, 1),
]
WEIGHTS = [1.0 / 3.0] + [1.0 / 18.0] * 6 + [1.0 / 36.0] * 12
EAST = [1, 7, 9, 11, 13]
WEST = [2, 8, 10, 12, 14]
UP = [3, 7, 10, 15, 17]
DOWN = [4, 8, 9, 16, 18]
OMEGA = 1.0 / 0.6
WALL_SPEED = 0.1
BOOST = 3.0 * WALL_SPEED / 36.0
NZ = 8
LANES = 128
GAP = 4
HALF = 64
BASE = 2


def lane_iota():
    return lax.broadcasted_iota(jnp.int32, (NZ, LANES), 1)


def roll_y(v, by):
    by = by % LANES
    return pltpu.roll(v, by, 1) if by else v


def roll_z(v, by):
    by = by % NZ
    return pltpu.roll(v, by, 0) if by else v


def moments(f):
    e = f[1] + f[11] + f[13]
    w = f[2] + f[12] + f[14]
    n = f[3] + f[15] + f[17]
    s = f[4] + f[16] + f[18]
    d79 = f[7] + f[9]
    d810 = f[8] + f[10]
    rho = ((f[0] + f[5]) + f[6]) + (e + w) + (n + s) + (d79 + d810)
    jx = (e - w) + (d79 - d810)
    jy = (n - s) + ((f[7] - f[9]) + (f[10] - f[8]))
    jz = (f[5] - f[6]) + ((f[11] - f[12]) + (f[14] - f[13])) + ((f[15] - f[16]) + (f[18] - f[17]))
    return rho, jx, jy, jz


def relax(rho, jx, jy, jz, f, wanted):
    inv = 1.0 / rho
    ux, uy, uz = jx * inv, jy * inv, jz * inv
    base = (rho - 1.5 * (jx * ux + jy * uy + jz * uz)) * (OMEGA / 36.0)
    keep = 1.0 - OMEGA
    post = {}
    done = set()
    for q in wanted:
        if q in done:
            continue
        cx, cy, cz = VELOCITY[q]
        if q == 0:
            post[0] = keep * f[0] + 12.0 * base
            continue
        opposite = VELOCITY.index((-cx, -cy, -cz))
        jc, uc = None, None
        for c, j, u in ((cx, jx, ux), (cy, jy, uy), (cz, jz, uz)):
            if c:
                if jc is None:
                    jc, uc = (j, u) if c > 0 else (-j, -u)
                else:
                    jc, uc = (jc + j, uc + u) if c > 0 else (jc - j, uc - u)
        scale = WEIGHTS[q] * 36.0
        even = base * scale if scale != 1.0 else base
        even = even + (jc * uc) * (4.5 * OMEGA * WEIGHTS[q])
        odd = jc * (3.0 * OMEGA * WEIGHTS[q])
        post[q] = keep * f[q] + (even + odd)
        done.add(q)
        if opposite in wanted:
            post[opposite] = keep * f[opposite] + (even - odd)
            done.add(opposite)
    return post


def classes(p, across):
    if across == "x":
        plus, minus = (1, 11, 13), (2, 12, 14)
    else:
        plus, minus = (3, 15, 17), (4, 16, 18)
    rising, falling = plus[1], plus[2]
    low, high = minus[1], minus[2]
    return [
        p[0] + p[5] + p[6],
        p[plus[0]] + p[rising] + p[falling],
        p[minus[0]] + p[low] + p[high],
        p[5] - p[6],
        p[rising] - p[falling],
        p[high] - p[low],
    ]


def column(ref, q, x, width):
    return ref[q, pl.ds(x, NZ, stride=width), :]


def pack_kernel(shears, width, f_ref, side_ref, gap_ref, own_ref, near_ref, far_ref):
    shear = lax.axis_index("shear")
    lane = lane_iota()
    boost_up = jnp.where(shear == shears - 1, -BOOST, 0.0).astype(jnp.float32)
    boost_down = jnp.where(shear == 0, BOOST, 0.0).astype(jnp.float32)
    here = [(lane >= x * GAP) & (lane < (x + 1) * GAP) for x in range(width)]
    edge = []
    for q in range(19):
        total = jnp.ones((NZ, LANES), jnp.float32)
        for x in range(width):
            total = jnp.where(here[x], roll_y(column(f_ref, q, x, width), x * GAP + 2), total)
        edge.append(total)
    rho, jx, jy, jz = moments(edge)
    post = relax(rho, jx, jy, jz, edge, range(19))
    post = {q: roll_z(post[q], VELOCITY[q][2]) for q in range(19)}
    sums = classes(post, "x")

    def groups(ghosts, outer, at, far):
        planes = [(g, at) for g in ghosts] + [(s, at) for s in sums] + [(o, far) for o in outer]
        vregs = []
        for v in range(2):
            total = None
            for half in range(2):
                for slot in range(GAP):
                    plane, row = planes[(v * 2 + half) * GAP + slot]
                    moved = roll_y(plane, half * HALF + slot - row)
                    if total is None:
                        total = moved
                    else:
                        inside = (lane >= half * HALF) & (lane < (half + 1) * HALF)
                        total = jnp.where(inside & (lane % GAP == slot), moved, total)
            vregs.append(total)
        return vregs

    ups = [post[q] + VELOCITY[q][0] * boost_up * rho if VELOCITY[q][0] else post[q] for q in UP]
    downs = [post[q] + VELOCITY[q][0] * boost_down * rho if VELOCITY[q][0] else post[q] for q in DOWN]
    up0, up1 = groups(ups, [post[q] for q in UP], 1, 0)
    down0, down1 = groups(downs, [post[q] for q in DOWN], 2, 3)
    low = lax.rem(shear, 2) == 0
    for at, (up, down) in enumerate(((up0, down0), (up1, down1))):
        side_ref[at] = jnp.where(low, up, down)
        gap_ref[at] = jnp.where(low, down, up)
    own_ref[0] = jnp.where(low, down0, up0)
    own_ref[1] = jnp.where(low, up0, down0)

    packs = []
    for near, far, lanes in ((width - 1, width - 2, EAST), (0, 1, WEST)):
        planes = []
        for at in (far, near):
            f = [column(f_ref, q, at, width) for q in range(19)]
            wanted = list(range(19)) if at == near else lanes
            post = relax(*moments(f), f, wanted)
            for q in wanted:
                post[q] = roll_y(roll_z(post[q], VELOCITY[q][2]), VELOCITY[q][1])
            planes += [post[q] for q in lanes]
        still, plus, minus, still_z, plus_z, minus_z = classes(post, "y")
        plus, plus_z = [jnp.where(lane == 0, 0.0, v) for v in (plus, plus_z)]
        minus, minus_z = [jnp.where(lane == LANES - 1, 0.0, v) for v in (minus, minus_z)]
        packs.append(planes + [still + (plus + minus), plus - minus, still_z + (plus_z + minus_z)])
    even = lax.rem(lax.axis_index("flow"), 2) == 0
    for i, (to_east, to_west) in enumerate(zip(*packs)):
        near_ref[i] = jnp.where(even, to_east, to_west)
        far_ref[i] = jnp.where(even, to_west, to_east)


def message_kernel(near_ref, far_ref, side_ref, own_ref, near_out, far_out):
    for out, planes in ((near_out, near_ref), (far_out, far_ref)):
        out[0:13] = planes[...]
        out[13:15] = side_ref[...]
        out[15] = own_ref[1]


def block_kernel(gap_ref, own_ref, out_ref):
    out_ref[0, 0:2] = gap_ref[...]
    out_ref[0, 2] = own_ref[0]


def join_kernel(count, mine_ref, theirs_ref, out_ref):
    mine = lax.rem(lax.div(lax.axis_index("flow"), count), 2)
    out_ref[pl.ds(mine * count, count)] = mine_ref[...]
    out_ref[pl.ds((1 - mine) * count, count)] = theirs_ref[...]


def local_kernel(width, f_ref, a_ref):
    def step(x):
        f = [column(f_ref, q, x, width) for q in range(19)]
        post = relax(*moments(f), f, range(19))
        for q in range(19):
            cx, cy, cz = VELOCITY[q]
            a_ref[q, x + 1 + cx] = roll_y(roll_z(post[q], cz), cy)

    pl.loop(0, width, unroll=2)(step)
    for q in range(19):
        cx = VELOCITY[q][0]
        zero = jnp.zeros((NZ, LANES), jnp.float32)
        for x in (0, 1, width, width + 1):
            if not 0 <= x - 1 - cx < width:
                a_ref[q, x] = zero


def finish_kernel(
    flows, shears, width, cells, weight, a_ref, mine_ref, theirs_ref, side_ref, own_ref,
    far_ref, near_ref, out_hbm, out_ref, sem_out,
):
    flow = lax.axis_index("flow")
    shear = lax.axis_index("shear")
    lane = lane_iota()
    total_x = flows * width
    even = lax.rem(flow, 2) == 0
    at_bottom = shear == 0
    at_top = shear == shears - 1
    half_flows = flows // 2
    my_half = lax.div(flow, half_flows)
    k1, k2 = cells[0], cells[1]
    frac = [weight[s].astype(jnp.float32) / WEIGHT_DENOM for s in range(2)]
    one, zero = jnp.float32(1.0), jnp.float32(0.0)

    def from_west(i):
        return jnp.where(even, far_ref[i], near_ref[i])

    def from_east(i):
        return jnp.where(even, near_ref[i], far_ref[i])

    def gathered(block, vreg):
        at = lax.rem(block, half_flows)
        return jnp.where(lax.div(block, half_flows) == my_half, mine_ref[at, vreg], theirs_ref[at, vreg])

    def window(start, shifted, vreg, half):
        first = lax.rem(flow * width + start - BASE + 2 * total_x, total_x)
        block = lax.div(first, width)
        skip = (first - block * width) * GAP
        beside = (from_west(13 + vreg), side_ref[vreg] if vreg < 2 else own_ref[1], from_east(13 + vreg))
        a, b, c = [
            jnp.where(shifted, gathered(lax.rem(block + k, flows), vreg), beside[k]) for k in range(3)
        ]
        if half:
            a, c = roll_y(a, HALF), roll_y(c, HALF)
        else:
            b = roll_y(b, HALF)
        both = jnp.where(lane < HALF, a, b)
        return pltpu.roll(jnp.where(lane >= skip, both, c), lax.rem(LANES - skip, LANES), 1)

    def side(upward):
        lanes = UP if upward else DOWN
        others = DOWN if upward else UP
        active = at_bottom if upward else at_top
        low = lax.rem(shear, 2) == 0
        shifted = low if upward else jnp.logical_not(low)

        def starts(k, low):
            return k if low else -k - 1

        def coefs(s, low):
            pair = (one - frac[s], frac[s]) if low else (frac[s], one - frac[s])
            return jnp.where(active, pair[0], one), jnp.where(active, pair[1], zero)

        def mixed(v, pair):
            return pair[0] * v + pair[1] * roll_y(v, -GAP)

        start1 = jnp.where(active, starts(k1, upward), 0)
        start2 = jnp.where(active, starts(k2, upward), 0)
        start3 = jnp.where(active, starts(k2, upward) + starts(k1, not upward), 0)
        near = [mixed(window(start1, shifted, 0, h), coefs(0, upward)) for h in range(2)]
        ghost1 = {q: (near[i // GAP], i % GAP) for i, q in enumerate(lanes)}
        packs = [None] + [window(start2, shifted, v, h) for v, h in ((0, 1), (1, 0), (1, 1))]
        pair3 = coefs(0, not upward)
        back = [mixed(window(start3, shifted, 2, h), pair3) for h in range(2)]

        def plane(at, by):
            return roll_y(packs[at // GAP], by * GAP - at % GAP)

        f = {}
        for i, q in enumerate(lanes):
            f[q] = plane(11 + i, VELOCITY[q][0])
        for i, q in enumerate(others):
            f[q] = roll_y(back[i // GAP], VELOCITY[q][0] * GAP - i % GAP)
        mid, plus, minus = plane(5, 0), plane(6, 1), plane(7, -1)
        midz, plusz, minusz = plane(8, 0), plane(9, 1), plane(10, -1)
        up = [f[q] for q in UP]
        down = [f[q] for q in DOWN]
        sum_up = up[0] + up[1] + up[2] + up[3] + up[4]
        sum_down = down[0] + down[1] + down[2] + down[3] + down[4]
        rho = (mid + plus + minus) + (sum_up + sum_down)
        jx = (plus - minus) + ((f[7] - f[10]) + (f[9] - f[8]))
        jy = sum_up - sum_down
        jz = (midz + plusz + minusz) + ((f[15] - f[17]) + (f[18] - f[16]))
        post = relax(rho, jx, jy, jz, f, lanes)
        boost = jnp.where(active, -BOOST if upward else BOOST, 0.0).astype(jnp.float32)
        pair2 = coefs(1, upward)
        ghost2 = {}
        for q in lanes:
            cx, _, cz = VELOCITY[q]
            p = post[q] + cx * boost * rho if cx else post[q]
            ghost2[q] = (roll_z(mixed(p, pair2), cz), 0)
        return ghost1, ghost2

    up1, up2 = side(True)
    down1, down2 = side(False)
    at_first = lane == 0
    at_last = lane == LANES - 1
    odd = lane % GAP == 1

    def pairs(ups, downs, streamed):
        found = []
        for u, d in zip(UP, DOWN):
            (gu, su), (gd, sd) = ups[u], downs[d]
            along = [VELOCITY[q][0] * GAP if streamed else 0 for q in (u, d)]
            found.append(jnp.where(odd, roll_y(gu, along[0] + 1 - su), roll_y(gd, along[1] - sd)))
        return found

    pairs1 = pairs(up1, down1, True)
    pairs2 = pairs(up2, down2, False)

    def beyond(found, x):
        return [roll_y(v, -1 - (x + BASE) * GAP) for v in found]

    def insert(v, q, edge):
        if q in UP:
            return jnp.where(at_first, edge[UP.index(q)], v)
        if q in DOWN:
            return jnp.where(at_last, edge[DOWN.index(q)], v)
        return v

    def arrived(q, x):
        if x == 0 and q in EAST:
            return from_west(5 + EAST.index(q))
        if x == width - 1 and q in WEST:
            return from_east(5 + WEST.index(q))
        return a_ref[q, x + 1]

    def put(post, x):
        edge = beyond(pairs2, x)
        for q in post:
            cx, cy, cz = VELOCITY[q]
            if 0 <= x + cx < width:
                v = insert(roll_y(roll_z(post[q], cz), cy), q, edge)
                out_ref[q, pl.ds(x + cx, NZ, stride=width), :] = v

    for x, halo, entering, leaving in ((-1, from_west, EAST, WEST), (width, from_east, WEST, EAST)):
        edge = beyond(pairs1, x)
        f = {q: insert(halo(i), q, edge) for i, q in enumerate(entering)}
        for q in leaving:
            f[q] = insert(a_ref[q, x + 1], q, edge)
        level, rising, falling = edge[0] + edge[3] + edge[4], edge[3], edge[4]
        more = jnp.where(at_first | at_last, level, 0.0)
        more_y = jnp.where(at_first, level, jnp.where(at_last, -level, 0.0))
        turn = rising - falling
        more_z = jnp.where(at_first, turn, jnp.where(at_last, -turn, 0.0))
        sum_e = f[1] + f[7] + f[9] + f[11] + f[13]
        sum_w = f[2] + f[8] + f[10] + f[12] + f[14]
        rho = (halo(10) + more) + (sum_e + sum_w)
        jx = sum_e - sum_w
        jy = (halo(11) + more_y) + ((f[7] - f[8]) + (f[10] - f[9]))
        jz = (halo(12) + more_z) + ((f[11] - f[12]) + (f[14] - f[13]))
        put(relax(rho, jx, jy, jz, f, entering), x)

    rows_of = (19, NZ, width, LANES)
    half = width // 2
    stores = [
        pltpu.make_async_copy(
            out_ref.reshape(rows_of).at[:, :, a : a + half], out_hbm.reshape(rows_of).at[:, :, a : a + half], sem_out.at[i]
        )
        for i, a in enumerate((0, half))
    ]
    for x in range(width):
        edge = beyond(pairs1, x)
        f = [insert(arrived(q, x), q, edge) for q in range(19)]
        post = relax(*moments(f), f, range(19))
        put(post, x)
        if x == half:
            stores[0].start()
    stores[1].start()
    for store in stores:
        store.wait()


def per_device(populations, le_cells, le_weight):
    width = populations.shape[2]
    height = populations.shape[3]
    flows = lax.axis_size("flow")
    shears = lax.axis_size("shear")
    assert populations.shape[:2] == (19, NZ) and height == LANES
    assert width * GAP == HALF and shears >= 4 and shears % 2 == 0 and flows >= 4 and flows & (flows - 1) == 0
    f32 = jnp.float32
    f = populations.reshape(19, NZ * width, height)
    vmem = pl.BlockSpec(memory_space=pltpu.VMEM)
    anyspace = pl.BlockSpec(memory_space=pl.ANY)
    hbm = pl.BlockSpec(memory_space=pltpu.HBM)
    smem = pl.BlockSpec(memory_space=pltpu.SMEM)
    params = pltpu.CompilerParams(vmem_limit_bytes=32 * 1024 * 1024)

    def body(kernel, *fixed):
        return lambda *refs: kernel(*fixed, *refs)

    def vregs(*counts):
        return jax.ShapeDtypeStruct((*counts, NZ, LANES), f32)

    def call(name, kernel, outs, *arrays):
        return pl.pallas_call(
            kernel, out_shape=outs, in_specs=[vmem] * len(arrays),
            out_specs=[vmem] * len(outs) if isinstance(outs, list) else vmem,
            compiler_params=params, name=name,
        )(*arrays)

    def swap(x, axis, partner):
        return lax.ppermute(x, axis, [(i, partner(i)) for i in range(lax.axis_size(axis))])

    side, gap, own, near, far = call(
        "pack", body(pack_kernel, shears, width), [vregs(2), vregs(2), vregs(2), vregs(13), vregs(13)], f
    )
    side = swap(side, "shear", lambda i: i ^ 1)
    gap = swap(gap, "shear", lambda i: (i - 1 + i % 2 * 2) % shears)
    mine = call("block", block_kernel, vregs(1, 3), gap, own)
    near, far = call("message", message_kernel, [vregs(16), vregs(16)], near, far, side, own)
    from_far = swap(far, "flow", lambda i: (i - 1 + i % 2 * 2) % flows)
    count = 1
    while True:
        theirs = swap(mine, "flow", lambda i: i ^ count)
        if count * 2 == flows:
            break
        mine = call("join", body(join_kernel, count), vregs(count * 2, 3), mine, theirs)
        count *= 2
    from_near = swap(near, "flow", lambda i: i ^ 1)
    streamed = pl.pallas_call(
        body(local_kernel, width),
        out_shape=jax.ShapeDtypeStruct((19, width + 2, NZ, LANES), f32),
        in_specs=[vmem],
        out_specs=vmem,
        compiler_params=params,
        cost_estimate=pl.CostEstimate(flops=8_000_000, bytes_accessed=2_700_000, transcendentals=0),
        name="local",
    )(f)
    out = pl.pallas_call(
        body(finish_kernel, flows, shears, width),
        out_shape=jax.ShapeDtypeStruct((19, NZ * width, LANES), f32),
        in_specs=[vmem] * 9,
        out_specs=anyspace,
        scratch_shapes=[
            pltpu.VMEM((19, NZ * width, LANES), f32),
            pltpu.SemaphoreType.DMA((2,)),
        ],
        compiler_params=params,
        name="finish",
    )(le_cells, le_weight, streamed, mine, theirs, side, own, from_far, from_near)
    return out.reshape(populations.shape)


def solution(mesh):
    return jax.shard_map(
        per_device,
        mesh=mesh,
        in_specs=(P(None, None, "flow", "shear"), P(), P()),
        out_specs=P(None, None, "flow", "shear"),
        check_vma=False,
    )
```

```python
import jax
import jax.numpy as jnp
from jax import lax
from jax.experimental import pallas as pl
from jax.experimental.pallas import tpu as pltpu
from jax.sharding import PartitionSpec as P

WEIGHT_DENOM = 256
VELOCITY = [
    (0, 0, 0),
    (1, 0, 0),
    (-1, 0, 0),
    (0, 1, 0),
    (0, -1, 0),
    (0, 0, 1),
    (0, 0, -1),
    (1, 1, 0),
    (-1, -1, 0),
    (1, -1, 0),
    (-1, 1, 0),
    (1, 0, 1),
    (-1, 0, -1),
    (1, 0, -1),
    (-1, 0, 1),
    (0, 1, 1),
    (0, -1, -1),
    (0, 1, -1),
    (0, -1, 1),
]
WEIGHTS = [1.0 / 3.0] + [1.0 / 18.0] * 6 + [1.0 / 36.0] * 12
EAST = [1, 7, 9, 11, 13]
WEST = [2, 8, 10, 12, 14]
UP = [3, 7, 10, 15, 17]
DOWN = [4, 8, 9, 16, 18]
OMEGA = 1.0 / 0.6
WALL_SPEED = 0.1
BOOST = 3.0 * WALL_SPEED / 36.0
NZ = 8
LANES = 128
GAP = 4
HALF = 64
BASE = 2


def lane_iota():
    return lax.broadcasted_iota(jnp.int32, (NZ, LANES), 1)


def roll_y(v, by):
    by = by % LANES
    return pltpu.roll(v, by, 1) if by else v


def roll_z(v, by):
    by = by % NZ
    return pltpu.roll(v, by, 0) if by else v


def moments(f):
    e = f[1] + f[11] + f[13]
    w = f[2] + f[12] + f[14]
    n = f[3] + f[15] + f[17]
    s = f[4] + f[16] + f[18]
    d79 = f[7] + f[9]
    d810 = f[8] + f[10]
    rho = ((f[0] + f[5]) + f[6]) + (e + w) + (n + s) + (d79 + d810)
    jx = (e - w) + (d79 - d810)
    jy = (n - s) + ((f[7] - f[9]) + (f[10] - f[8]))
    jz = (f[5] - f[6]) + ((f[11] - f[12]) + (f[14] - f[13])) + ((f[15] - f[16]) + (f[18] - f[17]))
    return rho, jx, jy, jz


def relax(rho, jx, jy, jz, f, wanted):
    inv = 1.0 / rho
    ux, uy, uz = jx * inv, jy * inv, jz * inv
    base = (rho - 1.5 * (jx * ux + jy * uy + jz * uz)) * (OMEGA / 36.0)
    keep = 1.0 - OMEGA
    post = {}
    done = set()
    for q in wanted:
        if q in done:
            continue
        cx, cy, cz = VELOCITY[q]
        if q == 0:
            post[0] = keep * f[0] + 12.0 * base
            continue
        opposite = VELOCITY.index((-cx, -cy, -cz))
        jc, uc = None, None
        for c, j, u in ((cx, jx, ux), (cy, jy, uy), (cz, jz, uz)):
            if c:
                if jc is None:
                    jc, uc = (j, u) if c > 0 else (-j, -u)
                else:
                    jc, uc = (jc + j, uc + u) if c > 0 else (jc - j, uc - u)
        scale = WEIGHTS[q] * 36.0
        even = base * scale if scale != 1.0 else base
        even = even + (jc * uc) * (4.5 * OMEGA * WEIGHTS[q])
        odd = jc * (3.0 * OMEGA * WEIGHTS[q])
        post[q] = keep * f[q] + (even + odd)
        done.add(q)
        if opposite in wanted:
            post[opposite] = keep * f[opposite] + (even - odd)
            done.add(opposite)
    return post


def classes(p, across):
    if across == "x":
        plus, minus = (1, 11, 13), (2, 12, 14)
    else:
        plus, minus = (3, 15, 17), (4, 16, 18)
    rising, falling = plus[1], plus[2]
    low, high = minus[1], minus[2]
    return [
        p[0] + p[5] + p[6],
        p[plus[0]] + p[rising] + p[falling],
        p[minus[0]] + p[low] + p[high],
        p[5] - p[6],
        p[rising] - p[falling],
        p[high] - p[low],
    ]


def gather_order(flows):
    return [1] + [2**k for k in range(flows.bit_length() - 2, 0, -1)]


def column(ref, q, x, width):
    return ref[q, pl.ds(x, NZ, stride=width), :]


def pack_kernel(shears, width, f_ref, side_ref, gap_ref, own_ref, near_ref, far_ref):
    shear = lax.axis_index("shear")
    lane = lane_iota()
    boost_up = jnp.where(shear == shears - 1, -BOOST, 0.0).astype(jnp.float32)
    boost_down = jnp.where(shear == 0, BOOST, 0.0).astype(jnp.float32)
    here = [(lane >= x * GAP) & (lane < (x + 1) * GAP) for x in range(width)]
    edge = []
    for q in range(19):
        total = jnp.ones((NZ, LANES), jnp.float32)
        for x in range(width):
            total = jnp.where(here[x], roll_y(column(f_ref, q, x, width), x * GAP + 2), total)
        edge.append(total)
    rho, jx, jy, jz = moments(edge)
    post = relax(rho, jx, jy, jz, edge, range(19))
    post = {q: roll_z(post[q], VELOCITY[q][2]) for q in range(19)}
    sums = classes(post, "x")

    def groups(ghosts, outer, at, far):
        planes = [(g, at) for g in ghosts] + [(s, at) for s in sums] + [(o, far) for o in outer]
        vregs = []
        for v in range(2):
            total = None
            for half in range(2):
                for slot in range(GAP):
                    plane, row = planes[(v * 2 + half) * GAP + slot]
                    moved = roll_y(plane, half * HALF + slot - row)
                    if total is None:
                        total = moved
                    else:
                        inside = (lane >= half * HALF) & (lane < (half + 1) * HALF)
                        total = jnp.where(inside & (lane % GAP == slot), moved, total)
            vregs.append(total)
        return vregs

    ups = [post[q] + VELOCITY[q][0] * boost_up * rho if VELOCITY[q][0] else post[q] for q in UP]
    downs = [post[q] + VELOCITY[q][0] * boost_down * rho if VELOCITY[q][0] else post[q] for q in DOWN]
    up0, up1 = groups(ups, [post[q] for q in UP], 1, 0)
    down0, down1 = groups(downs, [post[q] for q in DOWN], 2, 3)
    low = lax.rem(shear, 2) == 0
    for at, (up, down) in enumerate(((up0, down0), (up1, down1))):
        side_ref[at] = jnp.where(low, up, down)
        gap_ref[at] = jnp.where(low, down, up)
    own_ref[0] = jnp.where(low, down0, up0)
    own_ref[1] = jnp.where(low, up0, down0)

    packs = []
    for near, far, lanes in ((width - 1, width - 2, EAST), (0, 1, WEST)):
        planes = []
        for at in (far, near):
            f = [column(f_ref, q, at, width) for q in range(19)]
            wanted = list(range(19)) if at == near else lanes
            post = relax(*moments(f), f, wanted)
            for q in wanted:
                post[q] = roll_y(roll_z(post[q], VELOCITY[q][2]), VELOCITY[q][1])
            planes += [post[q] for q in lanes]
        still, plus, minus, still_z, plus_z, minus_z = classes(post, "y")
        plus, plus_z = [jnp.where(lane == 0, 0.0, v) for v in (plus, plus_z)]
        minus, minus_z = [jnp.where(lane == LANES - 1, 0.0, v) for v in (minus, minus_z)]
        packs.append(planes + [still + (plus + minus), plus - minus, still_z + (plus_z + minus_z)])
    even = lax.rem(lax.axis_index("flow"), 2) == 0
    for i, (to_east, to_west) in enumerate(zip(*packs)):
        near_ref[i] = jnp.where(even, to_east, to_west)
        far_ref[i] = jnp.where(even, to_west, to_east)


def message_kernel(near_ref, far_ref, side_ref, own_ref, near_out, far_out):
    for out, planes in ((near_out, near_ref), (far_out, far_ref)):
        out[0:13] = planes[...]
        out[13:15] = side_ref[...]
        out[15] = own_ref[1]


def block_kernel(gap_ref, own_ref, out_ref):
    out_ref[0, 0:2] = gap_ref[...]
    out_ref[0, 2] = own_ref[0]


def join_kernel(apart, mine_ref, theirs_ref, out_ref):
    count = mine_ref.shape[0]
    mine = lax.rem(lax.div(lax.axis_index("flow"), apart), 2)
    out_ref[pl.ds(mine * count, count)] = mine_ref[...]
    out_ref[pl.ds((1 - mine) * count, count)] = theirs_ref[...]


def local_kernel(width, f_ref, a_ref):
    def step(x):
        f = [column(f_ref, q, x, width) for q in range(19)]
        post = relax(*moments(f), f, range(19))
        for q in range(19):
            cx, cy, cz = VELOCITY[q]
            a_ref[q, x + 1 + cx] = roll_y(roll_z(post[q], cz), cy)

    pl.loop(0, width, unroll=2)(step)
    for q in range(19):
        cx = VELOCITY[q][0]
        zero = jnp.zeros((NZ, LANES), jnp.float32)
        for x in (0, 1, width, width + 1):
            if not 0 <= x - 1 - cx < width:
                a_ref[q, x] = zero


def finish_kernel(
    flows, shears, width, cells, weight, a_ref, mine_ref, theirs_ref, side_ref, own_ref,
    far_ref, near_ref, out_hbm, out_ref, sem_out,
):
    flow = lax.axis_index("flow")
    shear = lax.axis_index("shear")
    lane = lane_iota()
    total_x = flows * width
    even = lax.rem(flow, 2) == 0
    at_bottom = shear == 0
    at_top = shear == shears - 1
    k1, k2 = cells[0], cells[1]
    frac = [weight[s].astype(jnp.float32) / WEIGHT_DENOM for s in range(2)]
    one, zero = jnp.float32(1.0), jnp.float32(0.0)

    def from_west(i):
        return jnp.where(even, far_ref[i], near_ref[i])

    def from_east(i):
        return jnp.where(even, near_ref[i], far_ref[i])

    def gathered(block, vreg):
        *early, last = gather_order(flows)
        at = 0
        for place, apart in enumerate(early):
            at = at + lax.rem(lax.div(block, apart), 2) * 2**place
        same = lax.rem(lax.div(block, last), 2) == lax.rem(lax.div(flow, last), 2)
        return jnp.where(same, mine_ref[at, vreg], theirs_ref[at, vreg])

    def window(start, shifted, vreg, half):
        first = lax.rem(flow * width + start - BASE + 2 * total_x, total_x)
        block = lax.div(first, width)
        skip = (first - block * width) * GAP
        beside = (from_west(13 + vreg), side_ref[vreg] if vreg < 2 else own_ref[1], from_east(13 + vreg))
        a, b, c = [
            jnp.where(shifted, gathered(lax.rem(block + k, flows), vreg), beside[k]) for k in range(3)
        ]
        if half:
            a, c = roll_y(a, HALF), roll_y(c, HALF)
        else:
            b = roll_y(b, HALF)
        both = jnp.where(lane < HALF, a, b)
        return pltpu.roll(jnp.where(lane >= skip, both, c), lax.rem(LANES - skip, LANES), 1)

    def side(upward):
        lanes = UP if upward else DOWN
        others = DOWN if upward else UP
        active = at_bottom if upward else at_top
        low = lax.rem(shear, 2) == 0
        shifted = low if upward else jnp.logical_not(low)

        def starts(k, low):
            return k if low else -k - 1

        def coefs(s, low):
            pair = (one - frac[s], frac[s]) if low else (frac[s], one - frac[s])
            return jnp.where(active, pair[0], one), jnp.where(active, pair[1], zero)

        def mixed(v, pair):
            return pair[0] * v + pair[1] * roll_y(v, -GAP)

        start1 = jnp.where(active, starts(k1, upward), 0)
        start2 = jnp.where(active, starts(k2, upward), 0)
        start3 = jnp.where(active, starts(k2, upward) + starts(k1, not upward), 0)
        near = [mixed(window(start1, shifted, 0, h), coefs(0, upward)) for h in range(2)]
        ghost1 = {q: (near[i // GAP], i % GAP) for i, q in enumerate(lanes)}
        packs = [None] + [window(start2, shifted, v, h) for v, h in ((0, 1), (1, 0), (1, 1))]
        pair3 = coefs(0, not upward)
        back = [mixed(window(start3, shifted, 2, h), pair3) for h in range(2)]

        def plane(at, by):
            return roll_y(packs[at // GAP], by * GAP - at % GAP)

        f = {}
        for i, q in enumerate(lanes):
            f[q] = plane(11 + i, VELOCITY[q][0])
        for i, q in enumerate(others):
            f[q] = roll_y(back[i // GAP], VELOCITY[q][0] * GAP - i % GAP)
        mid, plus, minus = plane(5, 0), plane(6, 1), plane(7, -1)
        midz, plusz, minusz = plane(8, 0), plane(9, 1), plane(10, -1)
        up = [f[q] for q in UP]
        down = [f[q] for q in DOWN]
        sum_up = up[0] + up[1] + up[2] + up[3] + up[4]
        sum_down = down[0] + down[1] + down[2] + down[3] + down[4]
        rho = (mid + plus + minus) + (sum_up + sum_down)
        jx = (plus - minus) + ((f[7] - f[10]) + (f[9] - f[8]))
        jy = sum_up - sum_down
        jz = (midz + plusz + minusz) + ((f[15] - f[17]) + (f[18] - f[16]))
        post = relax(rho, jx, jy, jz, f, lanes)
        boost = jnp.where(active, -BOOST if upward else BOOST, 0.0).astype(jnp.float32)
        pair2 = coefs(1, upward)
        ghost2 = {}
        for q in lanes:
            cx, _, cz = VELOCITY[q]
            p = post[q] + cx * boost * rho if cx else post[q]
            ghost2[q] = (roll_z(mixed(p, pair2), cz), 0)
        return ghost1, ghost2

    up1, up2 = side(True)
    down1, down2 = side(False)
    at_first = lane == 0
    at_last = lane == LANES - 1
    odd = lane % GAP == 1

    def pairs(ups, downs, streamed):
        found = []
        for u, d in zip(UP, DOWN):
            (gu, su), (gd, sd) = ups[u], downs[d]
            along = [VELOCITY[q][0] * GAP if streamed else 0 for q in (u, d)]
            found.append(jnp.where(odd, roll_y(gu, along[0] + 1 - su), roll_y(gd, along[1] - sd)))
        return found

    pairs1 = pairs(up1, down1, True)
    pairs2 = pairs(up2, down2, False)

    def beyond(found, x):
        return [roll_y(v, -1 - (x + BASE) * GAP) for v in found]

    def insert(v, q, edge):
        if q in UP:
            return jnp.where(at_first, edge[UP.index(q)], v)
        if q in DOWN:
            return jnp.where(at_last, edge[DOWN.index(q)], v)
        return v

    def arrived(q, x):
        if x == 0 and q in EAST:
            return from_west(5 + EAST.index(q))
        if x == width - 1 and q in WEST:
            return from_east(5 + WEST.index(q))
        return a_ref[q, x + 1]

    def put(post, x):
        edge = beyond(pairs2, x)
        for q in post:
            cx, cy, cz = VELOCITY[q]
            if 0 <= x + cx < width:
                v = insert(roll_y(roll_z(post[q], cz), cy), q, edge)
                out_ref[q, pl.ds(x + cx, NZ, stride=width), :] = v

    for x, halo, entering, leaving in ((-1, from_west, EAST, WEST), (width, from_east, WEST, EAST)):
        edge = beyond(pairs1, x)
        f = {q: insert(halo(i), q, edge) for i, q in enumerate(entering)}
        for q in leaving:
            f[q] = insert(a_ref[q, x + 1], q, edge)
        level, rising, falling = edge[0] + edge[3] + edge[4], edge[3], edge[4]
        more = jnp.where(at_first | at_last, level, 0.0)
        more_y = jnp.where(at_first, level, jnp.where(at_last, -level, 0.0))
        turn = rising - falling
        more_z = jnp.where(at_first, turn, jnp.where(at_last, -turn, 0.0))
        sum_e = f[1] + f[7] + f[9] + f[11] + f[13]
        sum_w = f[2] + f[8] + f[10] + f[12] + f[14]
        rho = (halo(10) + more) + (sum_e + sum_w)
        jx = sum_e - sum_w
        jy = (halo(11) + more_y) + ((f[7] - f[8]) + (f[10] - f[9]))
        jz = (halo(12) + more_z) + ((f[11] - f[12]) + (f[14] - f[13]))
        put(relax(rho, jx, jy, jz, f, entering), x)

    rows_of = (19, NZ, width, LANES)
    half = width // 2
    stores = [
        pltpu.make_async_copy(
            out_ref.reshape(rows_of).at[:, :, a : a + half], out_hbm.reshape(rows_of).at[:, :, a : a + half], sem_out.at[i]
        )
        for i, a in enumerate((0, half))
    ]
    for x in range(width):
        edge = beyond(pairs1, x)
        f = [insert(arrived(q, x), q, edge) for q in range(19)]
        post = relax(*moments(f), f, range(19))
        put(post, x)
        if x == half:
            stores[0].start()
    stores[1].start()
    for store in stores:
        store.wait()


def per_device(populations, le_cells, le_weight):
    width = populations.shape[2]
    height = populations.shape[3]
    flows = lax.axis_size("flow")
    shears = lax.axis_size("shear")
    assert populations.shape[:2] == (19, NZ) and height == LANES
    assert width * GAP == HALF and shears >= 4 and shears % 2 == 0 and flows >= 4 and flows & (flows - 1) == 0
    f32 = jnp.float32
    f = populations.reshape(19, NZ * width, height)
    vmem = pl.BlockSpec(memory_space=pltpu.VMEM)
    anyspace = pl.BlockSpec(memory_space=pl.ANY)
    hbm = pl.BlockSpec(memory_space=pltpu.HBM)
    smem = pl.BlockSpec(memory_space=pltpu.SMEM)
    params = pltpu.CompilerParams(vmem_limit_bytes=32 * 1024 * 1024)

    def body(kernel, *fixed):
        return lambda *refs: kernel(*fixed, *refs)

    def vregs(*counts):
        return jax.ShapeDtypeStruct((*counts, NZ, LANES), f32)

    def call(name, kernel, outs, *arrays):
        return pl.pallas_call(
            kernel, out_shape=outs, in_specs=[vmem] * len(arrays),
            out_specs=[vmem] * len(outs) if isinstance(outs, list) else vmem,
            compiler_params=params, name=name,
        )(*arrays)

    def swap(x, axis, partner):
        return lax.ppermute(x, axis, [(i, partner(i)) for i in range(lax.axis_size(axis))])

    side, gap, own, near, far = call(
        "pack", body(pack_kernel, shears, width), [vregs(2), vregs(2), vregs(2), vregs(13), vregs(13)], f
    )
    side = swap(side, "shear", lambda i: i ^ 1)
    gap = swap(gap, "shear", lambda i: (i - 1 + i % 2 * 2) % shears)
    mine = call("block", block_kernel, vregs(1, 3), gap, own)
    near, far = call("message", message_kernel, [vregs(16), vregs(16)], near, far, side, own)
    from_far = swap(far, "flow", lambda i: (i - 1 + i % 2 * 2) % flows)
    *early, last = gather_order(flows)
    for apart in early:
        theirs = swap(mine, "flow", lambda i: i ^ apart)
        mine = call("join", body(join_kernel, apart), vregs(2 * mine.shape[0], 3), mine, theirs)
    theirs = swap(mine, "flow", lambda i: i ^ last)
    from_near = swap(near, "flow", lambda i: i ^ 1)
    streamed = pl.pallas_call(
        body(local_kernel, width),
        out_shape=jax.ShapeDtypeStruct((19, width + 2, NZ, LANES), f32),
        in_specs=[vmem],
        out_specs=vmem,
        compiler_params=params,
        cost_estimate=pl.CostEstimate(flops=8_000_000, bytes_accessed=2_700_000, transcendentals=0),
        name="local",
    )(f)
    out = pl.pallas_call(
        body(finish_kernel, flows, shears, width),
        out_shape=jax.ShapeDtypeStruct((19, NZ * width, LANES), f32),
        in_specs=[vmem] * 9,
        out_specs=anyspace,
        scratch_shapes=[
            pltpu.VMEM((19, NZ * width, LANES), f32),
            pltpu.SemaphoreType.DMA((2,)),
        ],
        compiler_params=params,
        name="finish",
    )(le_cells, le_weight, streamed, mine, theirs, side, own, from_far, from_near)
    return out.reshape(populations.shape)


def solution(mesh):
    return jax.shard_map(
        per_device,
        mesh=mesh,
        in_specs=(P(None, None, "flow", "shear"), P(), P()),
        out_specs=P(None, None, "flow", "shear"),
        check_vma=False,
    )
```

```python
import jax
import jax.numpy as jnp
from jax import lax
from jax.experimental import pallas as pl
from jax.experimental.pallas import tpu as pltpu
from jax.sharding import PartitionSpec as P

WEIGHT_DENOM = 256
VELOCITY = [
    (0, 0, 0),
    (1, 0, 0),
    (-1, 0, 0),
    (0, 1, 0),
    (0, -1, 0),
    (0, 0, 1),
    (0, 0, -1),
    (1, 1, 0),
    (-1, -1, 0),
    (1, -1, 0),
    (-1, 1, 0),
    (1, 0, 1),
    (-1, 0, -1),
    (1, 0, -1),
    (-1, 0, 1),
    (0, 1, 1),
    (0, -1, -1),
    (0, 1, -1),
    (0, -1, 1),
]
WEIGHTS = [1.0 / 3.0] + [1.0 / 18.0] * 6 + [1.0 / 36.0] * 12
EAST = [1, 7, 9, 11, 13]
WEST = [2, 8, 10, 12, 14]
LEVEL = [0, 1, 2, 5, 6, 11, 12, 13, 14]
UP = [3, 7, 10, 15, 17]
DOWN = [4, 8, 9, 16, 18]
OMEGA = 1.0 / 0.6
WALL_SPEED = 0.1
BOOST = 3.0 * WALL_SPEED / 36.0
NZ = 8
LANES = 128
GAP = 4
HALF = 64
BASE = 2


def lane_iota():
    return lax.broadcasted_iota(jnp.int32, (NZ, LANES), 1)


def roll_y(v, by):
    by = by % LANES
    return pltpu.roll(v, by, 1) if by else v


def roll_z(v, by):
    by = by % NZ
    return pltpu.roll(v, by, 0) if by else v


def moments(f):
    e = f[1] + f[11] + f[13]
    w = f[2] + f[12] + f[14]
    n = f[3] + f[15] + f[17]
    s = f[4] + f[16] + f[18]
    d79 = f[7] + f[9]
    d810 = f[8] + f[10]
    rho = ((f[0] + f[5]) + f[6]) + (e + w) + (n + s) + (d79 + d810)
    jx = (e - w) + (d79 - d810)
    jy = (n - s) + ((f[7] - f[9]) + (f[10] - f[8]))
    jz = (f[5] - f[6]) + ((f[11] - f[12]) + (f[14] - f[13])) + ((f[15] - f[16]) + (f[18] - f[17]))
    return rho, jx, jy, jz


def relax(rho, jx, jy, jz, f, wanted):
    inv = 1.0 / rho
    ux, uy, uz = jx * inv, jy * inv, jz * inv
    base = (rho - 1.5 * (jx * ux + jy * uy + jz * uz)) * (OMEGA / 36.0)
    keep = 1.0 - OMEGA
    post = {}
    done = set()
    for q in wanted:
        if q in done:
            continue
        cx, cy, cz = VELOCITY[q]
        if q == 0:
            post[0] = keep * f[0] + 12.0 * base
            continue
        opposite = VELOCITY.index((-cx, -cy, -cz))
        jc, uc = None, None
        for c, j, u in ((cx, jx, ux), (cy, jy, uy), (cz, jz, uz)):
            if c:
                if jc is None:
                    jc, uc = (j, u) if c > 0 else (-j, -u)
                else:
                    jc, uc = (jc + j, uc + u) if c > 0 else (jc - j, uc - u)
        scale = WEIGHTS[q] * 36.0
        even = base * scale if scale != 1.0 else base
        even = even + (jc * uc) * (4.5 * OMEGA * WEIGHTS[q])
        odd = jc * (3.0 * OMEGA * WEIGHTS[q])
        post[q] = keep * f[q] + (even + odd)
        done.add(q)
        if opposite in wanted:
            post[opposite] = keep * f[opposite] + (even - odd)
            done.add(opposite)
    return post


def classes(p, across):
    if across == "x":
        plus, minus = (1, 11, 13), (2, 12, 14)
    else:
        plus, minus = (3, 15, 17), (4, 16, 18)
    rising, falling = plus[1], plus[2]
    low, high = minus[1], minus[2]
    return [
        p[0] + p[5] + p[6],
        p[plus[0]] + p[rising] + p[falling],
        p[minus[0]] + p[low] + p[high],
        p[5] - p[6],
        p[rising] - p[falling],
        p[high] - p[low],
    ]


def gather_order(flows):
    return [1] + [2**k for k in range(flows.bit_length() - 2, 0, -1)]


def column(ref, q, x, width):
    return ref[q, pl.ds(x, NZ, stride=width), :]


def pack_kernel(shears, width, f_ref, side_ref, gap_ref, own_ref, near_ref, far_ref, edge_ref):
    shear = lax.axis_index("shear")
    lane = lane_iota()
    boost_up = jnp.where(shear == shears - 1, -BOOST, 0.0).astype(jnp.float32)
    boost_down = jnp.where(shear == 0, BOOST, 0.0).astype(jnp.float32)
    here = [(lane >= x * GAP) & (lane < (x + 1) * GAP) for x in range(width)]
    edge = []
    for q in range(19):
        total = jnp.ones((NZ, LANES), jnp.float32)
        for x in range(width):
            total = jnp.where(here[x], roll_y(column(f_ref, q, x, width), x * GAP + 2), total)
        edge.append(total)
    rho, jx, jy, jz = moments(edge)
    post = relax(rho, jx, jy, jz, edge, range(19))
    post = {q: roll_z(post[q], VELOCITY[q][2]) for q in range(19)}
    for q in range(19):
        edge_ref[q] = post[q]
    sums = classes(post, "x")

    def groups(ghosts, outer, at, far):
        planes = [(g, at) for g in ghosts] + [(s, at) for s in sums] + [(o, far) for o in outer]
        vregs = []
        for v in range(2):
            total = None
            for half in range(2):
                for slot in range(GAP):
                    plane, row = planes[(v * 2 + half) * GAP + slot]
                    moved = roll_y(plane, half * HALF + slot - row)
                    if total is None:
                        total = moved
                    else:
                        inside = (lane >= half * HALF) & (lane < (half + 1) * HALF)
                        total = jnp.where(inside & (lane % GAP == slot), moved, total)
            vregs.append(total)
        return vregs

    ups = [post[q] + VELOCITY[q][0] * boost_up * rho if VELOCITY[q][0] else post[q] for q in UP]
    downs = [post[q] + VELOCITY[q][0] * boost_down * rho if VELOCITY[q][0] else post[q] for q in DOWN]
    up0, up1 = groups(ups, [post[q] for q in UP], 1, 0)
    down0, down1 = groups(downs, [post[q] for q in DOWN], 2, 3)
    low = lax.rem(shear, 2) == 0
    for at, (up, down) in enumerate(((up0, down0), (up1, down1))):
        side_ref[at] = jnp.where(low, up, down)
        gap_ref[at] = jnp.where(low, down, up)
    own_ref[0] = jnp.where(low, down0, up0)
    own_ref[1] = jnp.where(low, up0, down0)

    packs = []
    for near, far, lanes in ((width - 1, width - 2, EAST), (0, 1, WEST)):
        planes = []
        for at in (far, near):
            f = [column(f_ref, q, at, width) for q in range(19)]
            wanted = list(range(19)) if at == near else lanes
            post = relax(*moments(f), f, wanted)
            for q in wanted:
                post[q] = roll_y(roll_z(post[q], VELOCITY[q][2]), VELOCITY[q][1])
            planes += [post[q] for q in lanes]
        still, plus, minus, still_z, plus_z, minus_z = classes(post, "y")
        plus, plus_z = [jnp.where(lane == 0, 0.0, v) for v in (plus, plus_z)]
        minus, minus_z = [jnp.where(lane == LANES - 1, 0.0, v) for v in (minus, minus_z)]
        packs.append(planes + [still + (plus + minus), plus - minus, still_z + (plus_z + minus_z)])
    even = lax.rem(lax.axis_index("flow"), 2) == 0
    for i, (to_east, to_west) in enumerate(zip(*packs)):
        near_ref[i] = jnp.where(even, to_east, to_west)
        far_ref[i] = jnp.where(even, to_west, to_east)


def message_kernel(near_ref, far_ref, side_ref, own_ref, near_out, far_out):
    for out, planes in ((near_out, near_ref), (far_out, far_ref)):
        out[0:13] = planes[...]
        out[13:15] = side_ref[...]
        out[15] = own_ref[1]


def block_kernel(gap_ref, own_ref, out_ref):
    out_ref[0, 0:2] = gap_ref[...]
    out_ref[0, 2] = own_ref[0]


def join_kernel(apart, mine_ref, theirs_ref, out_ref):
    count = mine_ref.shape[0]
    mine = lax.rem(lax.div(lax.axis_index("flow"), apart), 2)
    out_ref[pl.ds(mine * count, count)] = mine_ref[...]
    out_ref[pl.ds((1 - mine) * count, count)] = theirs_ref[...]


def local_kernel(width, f_ref, edge_ref, a_ref, inner_ref, own_ref):
    def first(x):
        f = [column(f_ref, q, x, width) for q in range(19)]
        post = relax(*moments(f), f, range(19))
        for q in range(19):
            cx, cy, cz = VELOCITY[q]
            a_ref[q, x + 1 + cx] = roll_y(roll_z(post[q], cz), cy)

    def second(x):
        f = [a_ref[q, x + 1] for q in range(19)]
        post = relax(*moments(f), f, range(19))
        for q in range(19):
            cx, cy, cz = VELOCITY[q]
            inner_ref[q, x + cx] = roll_y(roll_z(post[q], cz), cy)

    pl.loop(0, width, unroll=2)(first)
    pl.loop(1, width - 1, unroll=2)(second)
    for at, (lanes, row, far) in enumerate(((DOWN, 2, 3), (UP, 1, 0))):
        f = {}
        for q in LEVEL + lanes:
            f[q] = roll_y(edge_ref[q], (VELOCITY[q][0] + BASE) * GAP - (far if q in lanes else row))
        totals = [None] * 4
        for q in LEVEL + lanes:
            for k, c in enumerate((1,) + VELOCITY[q]):
                if c:
                    if totals[k] is None:
                        totals[k] = f[q] if c > 0 else -f[q]
                    else:
                        totals[k] = totals[k] + f[q] if c > 0 else totals[k] - f[q]
        for k, v in enumerate([f[q] for q in LEVEL] + totals):
            own_ref[at * 13 + k] = v


def finish_kernel(
    flows, shears, width, cells, weight, a_ref, inner_ref, within_ref, mine_ref, theirs_ref, side_ref, own_ref,
    far_ref, near_ref, out_hbm, out_ref, sem_out,
):
    flow = lax.axis_index("flow")
    shear = lax.axis_index("shear")
    lane = lane_iota()
    total_x = flows * width
    even = lax.rem(flow, 2) == 0
    at_bottom = shear == 0
    at_top = shear == shears - 1
    k1, k2 = cells[0], cells[1]
    frac = [weight[s].astype(jnp.float32) / WEIGHT_DENOM for s in range(2)]
    one, zero = jnp.float32(1.0), jnp.float32(0.0)

    def from_west(i):
        return jnp.where(even, far_ref[i], near_ref[i])

    def from_east(i):
        return jnp.where(even, near_ref[i], far_ref[i])

    def gathered(block, vreg):
        *early, last = gather_order(flows)
        at = 0
        for place, apart in enumerate(early):
            at = at + lax.rem(lax.div(block, apart), 2) * 2**place
        same = lax.rem(lax.div(block, last), 2) == lax.rem(lax.div(flow, last), 2)
        return jnp.where(same, mine_ref[at, vreg], theirs_ref[at, vreg])

    def window(start, shifted, vreg, half):
        first = lax.rem(flow * width + start - BASE + 2 * total_x, total_x)
        block = lax.div(first, width)
        skip = (first - block * width) * GAP
        beside = (from_west(13 + vreg), side_ref[vreg] if vreg < 2 else own_ref[1], from_east(13 + vreg))
        a, b, c = [
            jnp.where(shifted, gathered(lax.rem(block + k, flows), vreg), beside[k]) for k in range(3)
        ]
        if half:
            a, c = roll_y(a, HALF), roll_y(c, HALF)
        else:
            b = roll_y(b, HALF)
        both = jnp.where(lane < HALF, a, b)
        return pltpu.roll(jnp.where(lane >= skip, both, c), lax.rem(LANES - skip, LANES), 1)

    def side(upward):
        lanes = UP if upward else DOWN
        others = DOWN if upward else UP
        active = at_bottom if upward else at_top
        low = lax.rem(shear, 2) == 0
        shifted = low if upward else jnp.logical_not(low)

        def starts(k, low):
            return k if low else -k - 1

        def coefs(s, low):
            pair = (one - frac[s], frac[s]) if low else (frac[s], one - frac[s])
            return jnp.where(active, pair[0], one), jnp.where(active, pair[1], zero)

        def mixed(v, pair):
            return pair[0] * v + pair[1] * roll_y(v, -GAP)

        start1 = jnp.where(active, starts(k1, upward), 0)
        start2 = jnp.where(active, starts(k2, upward), 0)
        start3 = jnp.where(active, starts(k2, upward) + starts(k1, not upward), 0)
        near = [mixed(window(start1, shifted, 0, h), coefs(0, upward)) for h in range(2)]
        ghost1 = {q: (near[i // GAP], i % GAP) for i, q in enumerate(lanes)}
        packs = [None] + [window(start2, shifted, v, h) for v, h in ((0, 1), (1, 0), (1, 1))]
        pair3 = coefs(0, not upward)
        back = [mixed(window(start3, shifted, 2, h), pair3) for h in range(2)]

        def plane(at, by):
            return roll_y(packs[at // GAP], by * GAP - at % GAP)

        f = {}
        for i, q in enumerate(lanes):
            f[q] = plane(11 + i, VELOCITY[q][0])
        for i, q in enumerate(others):
            f[q] = roll_y(back[i // GAP], VELOCITY[q][0] * GAP - i % GAP)
        mid, plus, minus = plane(5, 0), plane(6, 1), plane(7, -1)
        midz, plusz, minusz = plane(8, 0), plane(9, 1), plane(10, -1)
        up = [f[q] for q in UP]
        down = [f[q] for q in DOWN]
        sum_up = up[0] + up[1] + up[2] + up[3] + up[4]
        sum_down = down[0] + down[1] + down[2] + down[3] + down[4]
        rho = (mid + plus + minus) + (sum_up + sum_down)
        jx = (plus - minus) + ((f[7] - f[10]) + (f[9] - f[8]))
        jy = sum_up - sum_down
        jz = (midz + plusz + minusz) + ((f[15] - f[17]) + (f[18] - f[16]))
        post = relax(rho, jx, jy, jz, f, lanes)
        boost = jnp.where(active, -BOOST if upward else BOOST, 0.0).astype(jnp.float32)
        pair2 = coefs(1, upward)
        ghost2 = {}
        for q in lanes:
            cx, _, cz = VELOCITY[q]
            p = post[q] + cx * boost * rho if cx else post[q]
            ghost2[q] = (roll_z(mixed(p, pair2), cz), 0)
        return ghost1, ghost2

    up1, up2 = side(True)
    down1, down2 = side(False)
    at_first = lane == 0
    at_last = lane == LANES - 1
    odd = lane % GAP == 1

    def pairs(ups, downs, streamed):
        found = []
        for u, d in zip(UP, DOWN):
            (gu, su), (gd, sd) = ups[u], downs[d]
            along = [VELOCITY[q][0] * GAP if streamed else 0 for q in (u, d)]
            found.append(jnp.where(odd, roll_y(gu, along[0] + 1 - su), roll_y(gd, along[1] - sd)))
        return found

    pairs1 = pairs(up1, down1, True)
    pairs2 = pairs(up2, down2, False)
    ghosts2 = {**up2, **down2}

    def beyond(found, x):
        return [roll_y(v, -1 - (x + BASE) * GAP) for v in found]

    def insert(v, q, edge):
        if q in UP:
            return jnp.where(at_first, edge[UP.index(q)], v)
        if q in DOWN:
            return jnp.where(at_last, edge[DOWN.index(q)], v)
        return v

    def arrived(q, x):
        if x == 0 and q in EAST:
            return from_west(5 + EAST.index(q))
        if x == width - 1 and q in WEST:
            return from_east(5 + WEST.index(q))
        return a_ref[q, x + 1]

    def put(post, x):
        edge = beyond(pairs2, x)
        for q in post:
            cx, cy, cz = VELOCITY[q]
            if 0 <= x + cx < width:
                v = insert(roll_y(roll_z(post[q], cz), cy), q, edge)
                out_ref[q, pl.ds(x + cx, NZ, stride=width), :] = v

    def halo_column(x):
        halo, entering, leaving = (from_west, EAST, WEST) if x < 0 else (from_east, WEST, EAST)
        edge = beyond(pairs1, x)
        f = {q: insert(halo(i), q, edge) for i, q in enumerate(entering)}
        for q in leaving:
            f[q] = insert(a_ref[q, x + 1], q, edge)
        level, rising, falling = edge[0] + edge[3] + edge[4], edge[3], edge[4]
        more = jnp.where(at_first | at_last, level, 0.0)
        more_y = jnp.where(at_first, level, jnp.where(at_last, -level, 0.0))
        turn = rising - falling
        more_z = jnp.where(at_first, turn, jnp.where(at_last, -turn, 0.0))
        sum_e = f[1] + f[7] + f[9] + f[11] + f[13]
        sum_w = f[2] + f[8] + f[10] + f[12] + f[14]
        rho = (halo(10) + more) + (sum_e + sum_w)
        jx = sum_e - sum_w
        jy = (halo(11) + more_y) + ((f[7] - f[8]) + (f[10] - f[9]))
        jz = (halo(12) + more_z) + ((f[11] - f[12]) + (f[14] - f[13]))
        put(relax(rho, jx, jy, jz, f, entering), x)

    patches = {}
    for at, lanes, slot in ((0, UP, 2), (1, DOWN, 1)):
        f = {q: within_ref[at * 13 + k] for k, q in enumerate(LEVEL)}
        for k, q in enumerate(lanes):
            f[q] = pairs1[k] if at else roll_y(pairs1[k], -1)
        totals = [within_ref[at * 13 + 9 + k] for k in range(4)]
        total = f[lanes[0]] + f[lanes[1]] + f[lanes[2]] + f[lanes[3]] + f[lanes[4]]
        if at:
            more = [total, f[9] - f[8], -total, f[18] - f[16]]
        else:
            more = [total, f[7] - f[10], total, f[15] - f[17]]
        post = relax(*[t + m for t, m in zip(totals, more)], f, LEVEL + lanes)
        for q in LEVEL + lanes:
            cx, cy, cz = VELOCITY[q]
            inside = roll_y(roll_z(post[q], cz), (cx - BASE) * GAP + slot + cy)
            if cy:
                outside = roll_y(ghosts2[q][0], (cx - BASE) * GAP + slot)
                patches[q] = jnp.where(lane % GAP == slot, outside, inside)
            elif at:
                patches[q] = jnp.where(lane % GAP == slot, inside, patches[q])
            else:
                patches[q] = inside
    mask = {1: lane < 2, -1: lane >= LANES - 2, 0: at_first | at_last}

    def merge(x):
        for q in range(19):
            cx, cy, cz = VELOCITY[q]
            if 1 <= x - cx < width - 1:
                moved = roll_y(patches[q], -(x * GAP + 2))
                out_ref[q, pl.ds(x, NZ, stride=width), :] = jnp.where(mask[cy], moved, inner_ref[q, x])

    rows_of = (19, NZ, width, LANES)
    half = width // 2
    stores = [
        pltpu.make_async_copy(
            out_ref.reshape(rows_of).at[:, :, a : a + half], out_hbm.reshape(rows_of).at[:, :, a : a + half], sem_out.at[i]
        )
        for i, a in enumerate((0, half))
    ]
    for store, rim, halo_at, xs in (
        (stores[0], 0, -1, range(half)),
        (stores[1], width - 1, width, range(half, width)),
    ):
        halo_column(halo_at)
        edge = beyond(pairs1, rim)
        f = [insert(arrived(q, rim), q, edge) for q in range(19)]
        put(relax(*moments(f), f, range(19)), rim)
        for x in xs:
            merge(x)
        store.start()
    for store in stores:
        store.wait()


def per_device(populations, le_cells, le_weight):
    width = populations.shape[2]
    height = populations.shape[3]
    flows = lax.axis_size("flow")
    shears = lax.axis_size("shear")
    assert populations.shape[:2] == (19, NZ) and height == LANES
    assert width * GAP == HALF and shears >= 4 and shears % 2 == 0 and flows >= 4 and flows & (flows - 1) == 0
    f32 = jnp.float32
    f = populations.reshape(19, NZ * width, height)
    vmem = pl.BlockSpec(memory_space=pltpu.VMEM)
    anyspace = pl.BlockSpec(memory_space=pl.ANY)
    hbm = pl.BlockSpec(memory_space=pltpu.HBM)
    smem = pl.BlockSpec(memory_space=pltpu.SMEM)
    params = pltpu.CompilerParams(vmem_limit_bytes=32 * 1024 * 1024)

    def body(kernel, *fixed):
        return lambda *refs: kernel(*fixed, *refs)

    def vregs(*counts):
        return jax.ShapeDtypeStruct((*counts, NZ, LANES), f32)

    def call(name, kernel, outs, *arrays):
        return pl.pallas_call(
            kernel, out_shape=outs, in_specs=[vmem] * len(arrays),
            out_specs=[vmem] * len(outs) if isinstance(outs, list) else vmem,
            compiler_params=params, name=name,
        )(*arrays)

    def swap(x, axis, partner):
        return lax.ppermute(x, axis, [(i, partner(i)) for i in range(lax.axis_size(axis))])

    side, gap, own, near, far, edge = call(
        "pack", body(pack_kernel, shears, width), [vregs(2), vregs(2), vregs(2), vregs(13), vregs(13), vregs(19)], f
    )
    side = swap(side, "shear", lambda i: i ^ 1)
    gap = swap(gap, "shear", lambda i: (i - 1 + i % 2 * 2) % shears)
    mine = call("block", block_kernel, vregs(1, 3), gap, own)
    near, far = call("message", message_kernel, [vregs(16), vregs(16)], near, far, side, own)
    from_far = swap(far, "flow", lambda i: (i - 1 + i % 2 * 2) % flows)
    *early, last = gather_order(flows)
    for apart in early:
        theirs = swap(mine, "flow", lambda i: i ^ apart)
        mine = call("join", body(join_kernel, apart), vregs(2 * mine.shape[0], 3), mine, theirs)
    theirs = swap(mine, "flow", lambda i: i ^ last)
    from_near = swap(near, "flow", lambda i: i ^ 1)
    streamed, inner, within = pl.pallas_call(
        body(local_kernel, width),
        out_shape=[vregs(19, width + 2), vregs(19, width), vregs(26)],
        in_specs=[vmem, vmem],
        out_specs=[vmem] * 3,
        compiler_params=params,
        cost_estimate=pl.CostEstimate(flops=16_000_000, bytes_accessed=4_000_000, transcendentals=0),
        name="local",
    )(f, edge)
    out = pl.pallas_call(
        body(finish_kernel, flows, shears, width),
        out_shape=jax.ShapeDtypeStruct((19, NZ * width, LANES), f32),
        in_specs=[vmem] * 11,
        out_specs=anyspace,
        scratch_shapes=[
            pltpu.VMEM((19, NZ * width, LANES), f32),
            pltpu.SemaphoreType.DMA((2,)),
        ],
        compiler_params=params,
        name="finish",
    )(le_cells, le_weight, streamed, inner, within, mine, theirs, side, own, from_far, from_near)
    return out.reshape(populations.shape)


def solution(mesh):
    return jax.shard_map(
        per_device,
        mesh=mesh,
        in_specs=(P(None, None, "flow", "shear"), P(), P()),
        out_specs=P(None, None, "flow", "shear"),
        check_vma=False,
    )
```

```python
import jax
import jax.numpy as jnp
from jax import lax
from jax.experimental import pallas as pl
from jax.experimental.pallas import tpu as pltpu
from jax.sharding import PartitionSpec as P

WEIGHT_DENOM = 256
VELOCITY = [
    (0, 0, 0),
    (1, 0, 0),
    (-1, 0, 0),
    (0, 1, 0),
    (0, -1, 0),
    (0, 0, 1),
    (0, 0, -1),
    (1, 1, 0),
    (-1, -1, 0),
    (1, -1, 0),
    (-1, 1, 0),
    (1, 0, 1),
    (-1, 0, -1),
    (1, 0, -1),
    (-1, 0, 1),
    (0, 1, 1),
    (0, -1, -1),
    (0, 1, -1),
    (0, -1, 1),
]
WEIGHTS = [1.0 / 3.0] + [1.0 / 18.0] * 6 + [1.0 / 36.0] * 12
EAST = [1, 7, 9, 11, 13]
WEST = [2, 8, 10, 12, 14]
UP = [3, 7, 10, 15, 17]
DOWN = [4, 8, 9, 16, 18]
OMEGA = 1.0 / 0.6
WALL_SPEED = 0.1
BOOST = 3.0 * WALL_SPEED / 36.0
NZ = 8
LANES = 128
GAP = 4
HALF = 64
BASE = 2


def lane_iota():
    return lax.broadcasted_iota(jnp.int32, (NZ, LANES), 1)


def roll_y(v, by):
    by = by % LANES
    return pltpu.roll(v, by, 1) if by else v


def roll_z(v, by):
    by = by % NZ
    return pltpu.roll(v, by, 0) if by else v


def moments(f):
    e = f[1] + f[11] + f[13]
    w = f[2] + f[12] + f[14]
    n = f[3] + f[15] + f[17]
    s = f[4] + f[16] + f[18]
    d79 = f[7] + f[9]
    d810 = f[8] + f[10]
    rho = ((f[0] + f[5]) + f[6]) + (e + w) + (n + s) + (d79 + d810)
    jx = (e - w) + (d79 - d810)
    jy = (n - s) + ((f[7] - f[9]) + (f[10] - f[8]))
    jz = (f[5] - f[6]) + ((f[11] - f[12]) + (f[14] - f[13])) + ((f[15] - f[16]) + (f[18] - f[17]))
    return rho, jx, jy, jz


def relax(rho, jx, jy, jz, f, wanted):
    inv = 1.0 / rho
    ux, uy, uz = jx * inv, jy * inv, jz * inv
    base = (rho - 1.5 * (jx * ux + jy * uy + jz * uz)) * (OMEGA / 36.0)
    keep = 1.0 - OMEGA
    post = {}
    done = set()
    for q in wanted:
        if q in done:
            continue
        cx, cy, cz = VELOCITY[q]
        if q == 0:
            post[0] = keep * f[0] + 12.0 * base
            continue
        opposite = VELOCITY.index((-cx, -cy, -cz))
        jc, uc = None, None
        for c, j, u in ((cx, jx, ux), (cy, jy, uy), (cz, jz, uz)):
            if c:
                if jc is None:
                    jc, uc = (j, u) if c > 0 else (-j, -u)
                else:
                    jc, uc = (jc + j, uc + u) if c > 0 else (jc - j, uc - u)
        scale = WEIGHTS[q] * 36.0
        even = base * scale if scale != 1.0 else base
        even = even + (jc * uc) * (4.5 * OMEGA * WEIGHTS[q])
        odd = jc * (3.0 * OMEGA * WEIGHTS[q])
        post[q] = keep * f[q] + (even + odd)
        done.add(q)
        if opposite in wanted:
            post[opposite] = keep * f[opposite] + (even - odd)
            done.add(opposite)
    return post


def classes(p, across):
    if across == "x":
        plus, minus = (1, 11, 13), (2, 12, 14)
    else:
        plus, minus = (3, 15, 17), (4, 16, 18)
    rising, falling = plus[1], plus[2]
    low, high = minus[1], minus[2]
    return [
        p[0] + p[5] + p[6],
        p[plus[0]] + p[rising] + p[falling],
        p[minus[0]] + p[low] + p[high],
        p[5] - p[6],
        p[rising] - p[falling],
        p[high] - p[low],
    ]


def gather_order(flows):
    return [1] + [2**k for k in range(flows.bit_length() - 2, 0, -1)]


def column(ref, q, x, width):
    return ref[q, pl.ds(x, NZ, stride=width), :]


def pack_kernel(shears, width, f_ref, side_ref, gap_ref, own_ref):
    shear = lax.axis_index("shear")
    lane = lane_iota()
    boost_up = jnp.where(shear == shears - 1, -BOOST, 0.0).astype(jnp.float32)
    boost_down = jnp.where(shear == 0, BOOST, 0.0).astype(jnp.float32)
    here = [(lane >= x * GAP) & (lane < (x + 1) * GAP) for x in range(width)]
    edge = []
    for q in range(19):
        total = jnp.ones((NZ, LANES), jnp.float32)
        for x in range(width):
            total = jnp.where(here[x], roll_y(column(f_ref, q, x, width), x * GAP + 2), total)
        edge.append(total)
    rho, jx, jy, jz = moments(edge)
    post = relax(rho, jx, jy, jz, edge, range(19))
    post = {q: roll_z(post[q], VELOCITY[q][2]) for q in range(19)}
    sums = classes(post, "x")

    def groups(ghosts, outer, at, far):
        planes = [(g, at) for g in ghosts] + [(s, at) for s in sums] + [(o, far) for o in outer]
        vregs = []
        for v in range(2):
            total = None
            for half in range(2):
                for slot in range(GAP):
                    plane, row = planes[(v * 2 + half) * GAP + slot]
                    moved = roll_y(plane, half * HALF + slot - row)
                    if total is None:
                        total = moved
                    else:
                        inside = (lane >= half * HALF) & (lane < (half + 1) * HALF)
                        total = jnp.where(inside & (lane % GAP == slot), moved, total)
            vregs.append(total)
        return vregs

    ups = [post[q] + VELOCITY[q][0] * boost_up * rho if VELOCITY[q][0] else post[q] for q in UP]
    downs = [post[q] + VELOCITY[q][0] * boost_down * rho if VELOCITY[q][0] else post[q] for q in DOWN]
    up0, up1 = groups(ups, [post[q] for q in UP], 1, 0)
    down0, down1 = groups(downs, [post[q] for q in DOWN], 2, 3)
    low = lax.rem(shear, 2) == 0
    for at, (up, down) in enumerate(((up0, down0), (up1, down1))):
        side_ref[at] = jnp.where(low, up, down)
        gap_ref[at] = jnp.where(low, down, up)
    own_ref[0] = jnp.where(low, down0, up0)
    own_ref[1] = jnp.where(low, up0, down0)


def columns_kernel(width, f_ref, near_ref, far_ref):
    lane = lane_iota()
    packs = []
    for near, far, lanes in ((width - 1, width - 2, EAST), (0, 1, WEST)):
        planes = []
        for at in (far, near):
            f = [column(f_ref, q, at, width) for q in range(19)]
            wanted = list(range(19)) if at == near else lanes
            post = relax(*moments(f), f, wanted)
            for q in wanted:
                post[q] = roll_y(roll_z(post[q], VELOCITY[q][2]), VELOCITY[q][1])
            planes += [post[q] for q in lanes]
        still, plus, minus, still_z, plus_z, minus_z = classes(post, "y")
        plus, plus_z = [jnp.where(lane == 0, 0.0, v) for v in (plus, plus_z)]
        minus, minus_z = [jnp.where(lane == LANES - 1, 0.0, v) for v in (minus, minus_z)]
        packs.append(planes + [still + (plus + minus), plus - minus, still_z + (plus_z + minus_z)])
    even = lax.rem(lax.axis_index("flow"), 2) == 0
    for i, (to_east, to_west) in enumerate(zip(*packs)):
        near_ref[i] = jnp.where(even, to_east, to_west)
        far_ref[i] = jnp.where(even, to_west, to_east)


def message_kernel(near_ref, far_ref, side_ref, own_ref, near_out, far_out):
    for out, planes in ((near_out, near_ref), (far_out, far_ref)):
        out[0:13] = planes[...]
        out[13:15] = side_ref[...]
        out[15] = own_ref[1]


def block_kernel(gap_ref, own_ref, ready_ref, out_ref):
    out_ref[0, 0:2] = gap_ref[...]
    out_ref[0, 2] = own_ref[0]


def join_kernel(apart, mine_ref, theirs_ref, out_ref):
    count = mine_ref.shape[0]
    mine = lax.rem(lax.div(lax.axis_index("flow"), apart), 2)
    out_ref[pl.ds(mine * count, count)] = mine_ref[...]
    out_ref[pl.ds((1 - mine) * count, count)] = theirs_ref[...]


def local_kernel(width, f_ref, a_ref):
    def step(x):
        f = [column(f_ref, q, x, width) for q in range(19)]
        post = relax(*moments(f), f, range(19))
        for q in range(19):
            cx, cy, cz = VELOCITY[q]
            a_ref[q, x + 1 + cx] = roll_y(roll_z(post[q], cz), cy)

    pl.loop(0, width, unroll=2)(step)
    for q in range(19):
        cx = VELOCITY[q][0]
        zero = jnp.zeros((NZ, LANES), jnp.float32)
        for x in (0, 1, width, width + 1):
            if not 0 <= x - 1 - cx < width:
                a_ref[q, x] = zero


def finish_kernel(
    flows, shears, width, cells, weight, a_ref, mine_ref, theirs_ref, side_ref, own_ref,
    far_ref, near_ref, out_hbm, out_ref, sem_out,
):
    flow = lax.axis_index("flow")
    shear = lax.axis_index("shear")
    lane = lane_iota()
    total_x = flows * width
    even = lax.rem(flow, 2) == 0
    at_bottom = shear == 0
    at_top = shear == shears - 1
    k1, k2 = cells[0], cells[1]
    frac = [weight[s].astype(jnp.float32) / WEIGHT_DENOM for s in range(2)]
    one, zero = jnp.float32(1.0), jnp.float32(0.0)

    def from_west(i):
        return jnp.where(even, far_ref[i], near_ref[i])

    def from_east(i):
        return jnp.where(even, near_ref[i], far_ref[i])

    def gathered(block, vreg):
        *early, last = gather_order(flows)
        at = 0
        for place, apart in enumerate(early):
            at = at + lax.rem(lax.div(block, apart), 2) * 2**place
        same = lax.rem(lax.div(block, last), 2) == lax.rem(lax.div(flow, last), 2)
        return jnp.where(same, mine_ref[at, vreg], theirs_ref[at, vreg])

    def window(start, shifted, vreg, half):
        first = lax.rem(flow * width + start - BASE + 2 * total_x, total_x)
        block = lax.div(first, width)
        skip = (first - block * width) * GAP
        beside = (from_west(13 + vreg), side_ref[vreg] if vreg < 2 else own_ref[1], from_east(13 + vreg))
        a, b, c = [
            jnp.where(shifted, gathered(lax.rem(block + k, flows), vreg), beside[k]) for k in range(3)
        ]
        if half:
            a, c = roll_y(a, HALF), roll_y(c, HALF)
        else:
            b = roll_y(b, HALF)
        both = jnp.where(lane < HALF, a, b)
        return pltpu.roll(jnp.where(lane >= skip, both, c), lax.rem(LANES - skip, LANES), 1)

    def side(upward):
        lanes = UP if upward else DOWN
        others = DOWN if upward else UP
        active = at_bottom if upward else at_top
        low = lax.rem(shear, 2) == 0
        shifted = low if upward else jnp.logical_not(low)

        def starts(k, low):
            return k if low else -k - 1

        def coefs(s, low):
            pair = (one - frac[s], frac[s]) if low else (frac[s], one - frac[s])
            return jnp.where(active, pair[0], one), jnp.where(active, pair[1], zero)

        def mixed(v, pair):
            return pair[0] * v + pair[1] * roll_y(v, -GAP)

        start1 = jnp.where(active, starts(k1, upward), 0)
        start2 = jnp.where(active, starts(k2, upward), 0)
        start3 = jnp.where(active, starts(k2, upward) + starts(k1, not upward), 0)
        near = [mixed(window(start1, shifted, 0, h), coefs(0, upward)) for h in range(2)]
        ghost1 = {q: (near[i // GAP], i % GAP) for i, q in enumerate(lanes)}
        packs = [None] + [window(start2, shifted, v, h) for v, h in ((0, 1), (1, 0), (1, 1))]
        pair3 = coefs(0, not upward)
        back = [mixed(window(start3, shifted, 2, h), pair3) for h in range(2)]

        def plane(at, by):
            return roll_y(packs[at // GAP], by * GAP - at % GAP)

        f = {}
        for i, q in enumerate(lanes):
            f[q] = plane(11 + i, VELOCITY[q][0])
        for i, q in enumerate(others):
            f[q] = roll_y(back[i // GAP], VELOCITY[q][0] * GAP - i % GAP)
        mid, plus, minus = plane(5, 0), plane(6, 1), plane(7, -1)
        midz, plusz, minusz = plane(8, 0), plane(9, 1), plane(10, -1)
        up = [f[q] for q in UP]
        down = [f[q] for q in DOWN]
        sum_up = up[0] + up[1] + up[2] + up[3] + up[4]
        sum_down = down[0] + down[1] + down[2] + down[3] + down[4]
        rho = (mid + plus + minus) + (sum_up + sum_down)
        jx = (plus - minus) + ((f[7] - f[10]) + (f[9] - f[8]))
        jy = sum_up - sum_down
        jz = (midz + plusz + minusz) + ((f[15] - f[17]) + (f[18] - f[16]))
        post = relax(rho, jx, jy, jz, f, lanes)
        boost = jnp.where(active, -BOOST if upward else BOOST, 0.0).astype(jnp.float32)
        pair2 = coefs(1, upward)
        ghost2 = {}
        for q in lanes:
            cx, _, cz = VELOCITY[q]
            p = post[q] + cx * boost * rho if cx else post[q]
            ghost2[q] = (roll_z(mixed(p, pair2), cz), 0)
        return ghost1, ghost2

    up1, up2 = side(True)
    down1, down2 = side(False)
    at_first = lane == 0
    at_last = lane == LANES - 1
    odd = lane % GAP == 1

    def pairs(ups, downs, streamed):
        found = []
        for u, d in zip(UP, DOWN):
            (gu, su), (gd, sd) = ups[u], downs[d]
            along = [VELOCITY[q][0] * GAP if streamed else 0 for q in (u, d)]
            found.append(jnp.where(odd, roll_y(gu, along[0] + 1 - su), roll_y(gd, along[1] - sd)))
        return found

    pairs1 = pairs(up1, down1, True)
    pairs2 = pairs(up2, down2, False)

    def beyond(found, x):
        return [roll_y(v, -1 - (x + BASE) * GAP) for v in found]

    def insert(v, q, edge):
        if q in UP:
            return jnp.where(at_first, edge[UP.index(q)], v)
        if q in DOWN:
            return jnp.where(at_last, edge[DOWN.index(q)], v)
        return v

    def arrived(q, x):
        if x == 0 and q in EAST:
            return from_west(5 + EAST.index(q))
        if x == width - 1 and q in WEST:
            return from_east(5 + WEST.index(q))
        return a_ref[q, x + 1]

    def put(post, x):
        edge = beyond(pairs2, x)
        for q in post:
            cx, cy, cz = VELOCITY[q]
            if 0 <= x + cx < width:
                v = insert(roll_y(roll_z(post[q], cz), cy), q, edge)
                out_ref[q, pl.ds(x + cx, NZ, stride=width), :] = v

    for x, halo, entering, leaving in ((-1, from_west, EAST, WEST), (width, from_east, WEST, EAST)):
        edge = beyond(pairs1, x)
        f = {q: insert(halo(i), q, edge) for i, q in enumerate(entering)}
        for q in leaving:
            f[q] = insert(a_ref[q, x + 1], q, edge)
        level, rising, falling = edge[0] + edge[3] + edge[4], edge[3], edge[4]
        more = jnp.where(at_first | at_last, level, 0.0)
        more_y = jnp.where(at_first, level, jnp.where(at_last, -level, 0.0))
        turn = rising - falling
        more_z = jnp.where(at_first, turn, jnp.where(at_last, -turn, 0.0))
        sum_e = f[1] + f[7] + f[9] + f[11] + f[13]
        sum_w = f[2] + f[8] + f[10] + f[12] + f[14]
        rho = (halo(10) + more) + (sum_e + sum_w)
        jx = sum_e - sum_w
        jy = (halo(11) + more_y) + ((f[7] - f[8]) + (f[10] - f[9]))
        jz = (halo(12) + more_z) + ((f[11] - f[12]) + (f[14] - f[13]))
        put(relax(rho, jx, jy, jz, f, entering), x)

    rows_of = (19, NZ, width, LANES)
    half = width // 2
    stores = [
        pltpu.make_async_copy(
            out_ref.reshape(rows_of).at[:, :, a : a + half], out_hbm.reshape(rows_of).at[:, :, a : a + half], sem_out.at[i]
        )
        for i, a in enumerate((0, half))
    ]
    for x in range(width):
        edge = beyond(pairs1, x)
        f = [insert(arrived(q, x), q, edge) for q in range(19)]
        post = relax(*moments(f), f, range(19))
        put(post, x)
        if x == half:
            stores[0].start()
    stores[1].start()
    for store in stores:
        store.wait()


def per_device(populations, le_cells, le_weight):
    width = populations.shape[2]
    height = populations.shape[3]
    flows = lax.axis_size("flow")
    shears = lax.axis_size("shear")
    assert populations.shape[:2] == (19, NZ) and height == LANES
    assert width * GAP == HALF and shears >= 4 and shears % 2 == 0 and flows >= 4 and flows & (flows - 1) == 0
    f32 = jnp.float32
    f = populations.reshape(19, NZ * width, height)
    vmem = pl.BlockSpec(memory_space=pltpu.VMEM)
    anyspace = pl.BlockSpec(memory_space=pl.ANY)
    hbm = pl.BlockSpec(memory_space=pltpu.HBM)
    smem = pl.BlockSpec(memory_space=pltpu.SMEM)
    params = pltpu.CompilerParams(vmem_limit_bytes=32 * 1024 * 1024)

    def body(kernel, *fixed):
        return lambda *refs: kernel(*fixed, *refs)

    def vregs(*counts):
        return jax.ShapeDtypeStruct((*counts, NZ, LANES), f32)

    def call(name, kernel, outs, *arrays):
        return pl.pallas_call(
            kernel, out_shape=outs, in_specs=[vmem] * len(arrays),
            out_specs=[vmem] * len(outs) if isinstance(outs, list) else vmem,
            compiler_params=params, name=name,
        )(*arrays)

    def swap(x, axis, partner):
        return lax.ppermute(x, axis, [(i, partner(i)) for i in range(lax.axis_size(axis))])

    side, gap, own = call("pack", body(pack_kernel, shears, width), [vregs(2)] * 3, f)
    near, far = call("columns", body(columns_kernel, width), [vregs(13)] * 2, f)
    side = swap(side, "shear", lambda i: i ^ 1)
    gap = swap(gap, "shear", lambda i: (i - 1 + i % 2 * 2) % shears)
    mine = call("block", block_kernel, vregs(1, 3), gap, own, near)
    near, far = call("message", message_kernel, [vregs(16), vregs(16)], near, far, side, own)
    from_far = swap(far, "flow", lambda i: (i - 1 + i % 2 * 2) % flows)
    *early, last = gather_order(flows)
    for apart in early:
        theirs = swap(mine, "flow", lambda i: i ^ apart)
        mine = call("join", body(join_kernel, apart), vregs(2 * mine.shape[0], 3), mine, theirs)
    theirs = swap(mine, "flow", lambda i: i ^ last)
    from_near = swap(near, "flow", lambda i: i ^ 1)
    streamed = pl.pallas_call(
        body(local_kernel, width),
        out_shape=jax.ShapeDtypeStruct((19, width + 2, NZ, LANES), f32),
        in_specs=[vmem],
        out_specs=vmem,
        compiler_params=params,
        cost_estimate=pl.CostEstimate(flops=8_000_000, bytes_accessed=2_700_000, transcendentals=0),
        name="local",
    )(f)
    out = pl.pallas_call(
        body(finish_kernel, flows, shears, width),
        out_shape=jax.ShapeDtypeStruct((19, NZ * width, LANES), f32),
        in_specs=[vmem] * 9,
        out_specs=anyspace,
        scratch_shapes=[
            pltpu.VMEM((19, NZ * width, LANES), f32),
            pltpu.SemaphoreType.DMA((2,)),
        ],
        compiler_params=params,
        name="finish",
    )(le_cells, le_weight, streamed, mine, theirs, side, own, from_far, from_near)
    return out.reshape(populations.shape)


def solution(mesh):
    return jax.shard_map(
        per_device,
        mesh=mesh,
        in_specs=(P(None, None, "flow", "shear"), P(), P()),
        out_specs=P(None, None, "flow", "shear"),
        check_vma=False,
    )
```

```python
import jax
import jax.numpy as jnp
from jax import lax
from jax.experimental import pallas as pl
from jax.experimental.pallas import tpu as pltpu
from jax.sharding import PartitionSpec as P

WEIGHT_DENOM = 256
VELOCITY = [
    (0, 0, 0),
    (1, 0, 0),
    (-1, 0, 0),
    (0, 1, 0),
    (0, -1, 0),
    (0, 0, 1),
    (0, 0, -1),
    (1, 1, 0),
    (-1, -1, 0),
    (1, -1, 0),
    (-1, 1, 0),
    (1, 0, 1),
    (-1, 0, -1),
    (1, 0, -1),
    (-1, 0, 1),
    (0, 1, 1),
    (0, -1, -1),
    (0, 1, -1),
    (0, -1, 1),
]
WEIGHTS = [1.0 / 3.0] + [1.0 / 18.0] * 6 + [1.0 / 36.0] * 12
EAST = [1, 7, 9, 11, 13]
WEST = [2, 8, 10, 12, 14]
UP = [3, 7, 10, 15, 17]
DOWN = [4, 8, 9, 16, 18]
OMEGA = 1.0 / 0.6
WALL_SPEED = 0.1
BOOST = 3.0 * WALL_SPEED / 36.0
NZ = 8
LANES = 128
GAP = 4
HALF = 64
BASE = 2


def lane_iota():
    return lax.broadcasted_iota(jnp.int32, (NZ, LANES), 1)


def roll_y(v, by):
    by = by % LANES
    return pltpu.roll(v, by, 1) if by else v


def roll_z(v, by):
    by = by % NZ
    return pltpu.roll(v, by, 0) if by else v


def moments(f):
    e = f[1] + f[11] + f[13]
    w = f[2] + f[12] + f[14]
    n = f[3] + f[15] + f[17]
    s = f[4] + f[16] + f[18]
    d79 = f[7] + f[9]
    d810 = f[8] + f[10]
    rho = ((f[0] + f[5]) + f[6]) + (e + w) + (n + s) + (d79 + d810)
    jx = (e - w) + (d79 - d810)
    jy = (n - s) + ((f[7] - f[9]) + (f[10] - f[8]))
    jz = (f[5] - f[6]) + ((f[11] - f[12]) + (f[14] - f[13])) + ((f[15] - f[16]) + (f[18] - f[17]))
    return rho, jx, jy, jz


def relax(rho, jx, jy, jz, f, wanted):
    inv = 1.0 / rho
    ux, uy, uz = jx * inv, jy * inv, jz * inv
    base = (rho - 1.5 * (jx * ux + jy * uy + jz * uz)) * (OMEGA / 36.0)
    keep = 1.0 - OMEGA
    post = {}
    done = set()
    for q in wanted:
        if q in done:
            continue
        cx, cy, cz = VELOCITY[q]
        if q == 0:
            post[0] = keep * f[0] + 12.0 * base
            continue
        opposite = VELOCITY.index((-cx, -cy, -cz))
        jc, uc = None, None
        for c, j, u in ((cx, jx, ux), (cy, jy, uy), (cz, jz, uz)):
            if c:
                if jc is None:
                    jc, uc = (j, u) if c > 0 else (-j, -u)
                else:
                    jc, uc = (jc + j, uc + u) if c > 0 else (jc - j, uc - u)
        scale = WEIGHTS[q] * 36.0
        even = base * scale if scale != 1.0 else base
        even = even + (jc * uc) * (4.5 * OMEGA * WEIGHTS[q])
        odd = jc * (3.0 * OMEGA * WEIGHTS[q])
        post[q] = keep * f[q] + (even + odd)
        done.add(q)
        if opposite in wanted:
            post[opposite] = keep * f[opposite] + (even - odd)
            done.add(opposite)
    return post


def classes(p, across):
    if across == "x":
        plus, minus = (1, 11, 13), (2, 12, 14)
    else:
        plus, minus = (3, 15, 17), (4, 16, 18)
    rising, falling = plus[1], plus[2]
    low, high = minus[1], minus[2]
    return [
        p[0] + p[5] + p[6],
        p[plus[0]] + p[rising] + p[falling],
        p[minus[0]] + p[low] + p[high],
        p[5] - p[6],
        p[rising] - p[falling],
        p[high] - p[low],
    ]


def gather_order(flows):
    return [1] + [2**k for k in range(flows.bit_length() - 2, 0, -1)]


def column(ref, q, x, width):
    return ref[q, pl.ds(x, NZ, stride=width), :]


def pack_kernel(shears, width, f_hbm, side_ref, gap_ref, own_ref, near_ref, far_ref, f_ref, sems):
    cuts = [0, 10, 19]
    copies = [
        pltpu.make_async_copy(f_hbm.at[a:b], f_ref.at[a:b], sems.at[i])
        for i, (a, b) in enumerate(zip(cuts, cuts[1:]))
    ]
    for copy in copies:
        copy.start()
    shear = lax.axis_index("shear")
    lane = lane_iota()
    boost_up = jnp.where(shear == shears - 1, -BOOST, 0.0).astype(jnp.float32)
    boost_down = jnp.where(shear == 0, BOOST, 0.0).astype(jnp.float32)
    here = [(lane >= x * GAP) & (lane < (x + 1) * GAP) for x in range(width)]
    edge = []
    for q in range(19):
        if q in cuts:
            copies[cuts.index(q)].wait()
        total = jnp.ones((NZ, LANES), jnp.float32)
        for x in range(width):
            total = jnp.where(here[x], roll_y(column(f_ref, q, x, width), x * GAP + 2), total)
        edge.append(total)
    rho, jx, jy, jz = moments(edge)
    post = relax(rho, jx, jy, jz, edge, range(19))
    post = {q: roll_z(post[q], VELOCITY[q][2]) for q in range(19)}
    sums = classes(post, "x")

    def groups(ghosts, outer, at, far):
        planes = [(g, at) for g in ghosts] + [(s, at) for s in sums] + [(o, far) for o in outer]
        vregs = []
        for v in range(2):
            total = None
            for half in range(2):
                for slot in range(GAP):
                    plane, row = planes[(v * 2 + half) * GAP + slot]
                    moved = roll_y(plane, half * HALF + slot - row)
                    if total is None:
                        total = moved
                    else:
                        inside = (lane >= half * HALF) & (lane < (half + 1) * HALF)
                        total = jnp.where(inside & (lane % GAP == slot), moved, total)
            vregs.append(total)
        return vregs

    ups = [post[q] + VELOCITY[q][0] * boost_up * rho if VELOCITY[q][0] else post[q] for q in UP]
    downs = [post[q] + VELOCITY[q][0] * boost_down * rho if VELOCITY[q][0] else post[q] for q in DOWN]
    up0, up1 = groups(ups, [post[q] for q in UP], 1, 0)
    down0, down1 = groups(downs, [post[q] for q in DOWN], 2, 3)
    low = lax.rem(shear, 2) == 0
    for at, (up, down) in enumerate(((up0, down0), (up1, down1))):
        side_ref[at] = jnp.where(low, up, down)
        gap_ref[at] = jnp.where(low, down, up)
    own_ref[0] = jnp.where(low, down0, up0)
    own_ref[1] = jnp.where(low, up0, down0)

    packs = []
    for near, far, lanes in ((width - 1, width - 2, EAST), (0, 1, WEST)):
        planes = []
        for at in (far, near):
            f = [column(f_ref, q, at, width) for q in range(19)]
            wanted = list(range(19)) if at == near else lanes
            post = relax(*moments(f), f, wanted)
            for q in wanted:
                post[q] = roll_y(roll_z(post[q], VELOCITY[q][2]), VELOCITY[q][1])
            planes += [post[q] for q in lanes]
        still, plus, minus, still_z, plus_z, minus_z = classes(post, "y")
        plus, plus_z = [jnp.where(lane == 0, 0.0, v) for v in (plus, plus_z)]
        minus, minus_z = [jnp.where(lane == LANES - 1, 0.0, v) for v in (minus, minus_z)]
        packs.append(planes + [still + (plus + minus), plus - minus, still_z + (plus_z + minus_z)])
    even = lax.rem(lax.axis_index("flow"), 2) == 0
    for i, (to_east, to_west) in enumerate(zip(*packs)):
        near_ref[i] = jnp.where(even, to_east, to_west)
        far_ref[i] = jnp.where(even, to_west, to_east)


def message_kernel(near_ref, far_ref, side_ref, own_ref, near_out, far_out):
    for out, planes in ((near_out, near_ref), (far_out, far_ref)):
        out[0:13] = planes[...]
        out[13:15] = side_ref[...]
        out[15] = own_ref[1]


def block_kernel(gap_ref, own_ref, out_ref):
    out_ref[0, 0:2] = gap_ref[...]
    out_ref[0, 2] = own_ref[0]


def join_kernel(apart, mine_ref, theirs_ref, out_ref):
    count = mine_ref.shape[0]
    mine = lax.rem(lax.div(lax.axis_index("flow"), apart), 2)
    out_ref[pl.ds(mine * count, count)] = mine_ref[...]
    out_ref[pl.ds((1 - mine) * count, count)] = theirs_ref[...]


def local_kernel(width, f_ref, a_ref):
    def step(x):
        f = [column(f_ref, q, x, width) for q in range(19)]
        post = relax(*moments(f), f, range(19))
        for q in range(19):
            cx, cy, cz = VELOCITY[q]
            a_ref[q, x + 1 + cx] = roll_y(roll_z(post[q], cz), cy)

    pl.loop(0, width, unroll=2)(step)
    for q in range(19):
        cx = VELOCITY[q][0]
        zero = jnp.zeros((NZ, LANES), jnp.float32)
        for x in (0, 1, width, width + 1):
            if not 0 <= x - 1 - cx < width:
                a_ref[q, x] = zero


def finish_kernel(
    flows, shears, width, cells, weight, a_ref, mine_ref, theirs_ref, side_ref, own_ref,
    far_ref, near_ref, out_hbm, out_ref, sem_out,
):
    flow = lax.axis_index("flow")
    shear = lax.axis_index("shear")
    lane = lane_iota()
    total_x = flows * width
    even = lax.rem(flow, 2) == 0
    at_bottom = shear == 0
    at_top = shear == shears - 1
    k1, k2 = cells[0], cells[1]
    frac = [weight[s].astype(jnp.float32) / WEIGHT_DENOM for s in range(2)]
    one, zero = jnp.float32(1.0), jnp.float32(0.0)

    def from_west(i):
        return jnp.where(even, far_ref[i], near_ref[i])

    def from_east(i):
        return jnp.where(even, near_ref[i], far_ref[i])

    def gathered(block, vreg):
        *early, last = gather_order(flows)
        at = 0
        for place, apart in enumerate(early):
            at = at + lax.rem(lax.div(block, apart), 2) * 2**place
        same = lax.rem(lax.div(block, last), 2) == lax.rem(lax.div(flow, last), 2)
        return jnp.where(same, mine_ref[at, vreg], theirs_ref[at, vreg])

    def window(start, shifted, vreg, half):
        first = lax.rem(flow * width + start - BASE + 2 * total_x, total_x)
        block = lax.div(first, width)
        skip = (first - block * width) * GAP
        beside = (from_west(13 + vreg), side_ref[vreg] if vreg < 2 else own_ref[1], from_east(13 + vreg))
        a, b, c = [
            jnp.where(shifted, gathered(lax.rem(block + k, flows), vreg), beside[k]) for k in range(3)
        ]
        if half:
            a, c = roll_y(a, HALF), roll_y(c, HALF)
        else:
            b = roll_y(b, HALF)
        both = jnp.where(lane < HALF, a, b)
        return pltpu.roll(jnp.where(lane >= skip, both, c), lax.rem(LANES - skip, LANES), 1)

    def side(upward):
        lanes = UP if upward else DOWN
        others = DOWN if upward else UP
        active = at_bottom if upward else at_top
        low = lax.rem(shear, 2) == 0
        shifted = low if upward else jnp.logical_not(low)

        def starts(k, low):
            return k if low else -k - 1

        def coefs(s, low):
            pair = (one - frac[s], frac[s]) if low else (frac[s], one - frac[s])
            return jnp.where(active, pair[0], one), jnp.where(active, pair[1], zero)

        def mixed(v, pair):
            return pair[0] * v + pair[1] * roll_y(v, -GAP)

        start1 = jnp.where(active, starts(k1, upward), 0)
        start2 = jnp.where(active, starts(k2, upward), 0)
        start3 = jnp.where(active, starts(k2, upward) + starts(k1, not upward), 0)
        near = [mixed(window(start1, shifted, 0, h), coefs(0, upward)) for h in range(2)]
        ghost1 = {q: (near[i // GAP], i % GAP) for i, q in enumerate(lanes)}
        packs = [None] + [window(start2, shifted, v, h) for v, h in ((0, 1), (1, 0), (1, 1))]
        pair3 = coefs(0, not upward)
        back = [mixed(window(start3, shifted, 2, h), pair3) for h in range(2)]

        def plane(at, by):
            return roll_y(packs[at // GAP], by * GAP - at % GAP)

        f = {}
        for i, q in enumerate(lanes):
            f[q] = plane(11 + i, VELOCITY[q][0])
        for i, q in enumerate(others):
            f[q] = roll_y(back[i // GAP], VELOCITY[q][0] * GAP - i % GAP)
        mid, plus, minus = plane(5, 0), plane(6, 1), plane(7, -1)
        midz, plusz, minusz = plane(8, 0), plane(9, 1), plane(10, -1)
        up = [f[q] for q in UP]
        down = [f[q] for q in DOWN]
        sum_up = up[0] + up[1] + up[2] + up[3] + up[4]
        sum_down = down[0] + down[1] + down[2] + down[3] + down[4]
        rho = (mid + plus + minus) + (sum_up + sum_down)
        jx = (plus - minus) + ((f[7] - f[10]) + (f[9] - f[8]))
        jy = sum_up - sum_down
        jz = (midz + plusz + minusz) + ((f[15] - f[17]) + (f[18] - f[16]))
        post = relax(rho, jx, jy, jz, f, lanes)
        boost = jnp.where(active, -BOOST if upward else BOOST, 0.0).astype(jnp.float32)
        pair2 = coefs(1, upward)
        ghost2 = {}
        for q in lanes:
            cx, _, cz = VELOCITY[q]
            p = post[q] + cx * boost * rho if cx else post[q]
            ghost2[q] = (roll_z(mixed(p, pair2), cz), 0)
        return ghost1, ghost2

    up1, up2 = side(True)
    down1, down2 = side(False)
    at_first = lane == 0
    at_last = lane == LANES - 1
    odd = lane % GAP == 1

    def pairs(ups, downs, streamed):
        found = []
        for u, d in zip(UP, DOWN):
            (gu, su), (gd, sd) = ups[u], downs[d]
            along = [VELOCITY[q][0] * GAP if streamed else 0 for q in (u, d)]
            found.append(jnp.where(odd, roll_y(gu, along[0] + 1 - su), roll_y(gd, along[1] - sd)))
        return found

    pairs1 = pairs(up1, down1, True)
    pairs2 = pairs(up2, down2, False)

    def beyond(found, x):
        return [roll_y(v, -1 - (x + BASE) * GAP) for v in found]

    def insert(v, q, edge):
        if q in UP:
            return jnp.where(at_first, edge[UP.index(q)], v)
        if q in DOWN:
            return jnp.where(at_last, edge[DOWN.index(q)], v)
        return v

    def arrived(q, x):
        if x == 0 and q in EAST:
            return from_west(5 + EAST.index(q))
        if x == width - 1 and q in WEST:
            return from_east(5 + WEST.index(q))
        return a_ref[q, x + 1]

    def put(post, x):
        edge = beyond(pairs2, x)
        for q in post:
            cx, cy, cz = VELOCITY[q]
            if 0 <= x + cx < width:
                v = insert(roll_y(roll_z(post[q], cz), cy), q, edge)
                out_ref[q, pl.ds(x + cx, NZ, stride=width), :] = v

    for x, halo, entering, leaving in ((-1, from_west, EAST, WEST), (width, from_east, WEST, EAST)):
        edge = beyond(pairs1, x)
        f = {q: insert(halo(i), q, edge) for i, q in enumerate(entering)}
        for q in leaving:
            f[q] = insert(a_ref[q, x + 1], q, edge)
        level, rising, falling = edge[0] + edge[3] + edge[4], edge[3], edge[4]
        more = jnp.where(at_first | at_last, level, 0.0)
        more_y = jnp.where(at_first, level, jnp.where(at_last, -level, 0.0))
        turn = rising - falling
        more_z = jnp.where(at_first, turn, jnp.where(at_last, -turn, 0.0))
        sum_e = f[1] + f[7] + f[9] + f[11] + f[13]
        sum_w = f[2] + f[8] + f[10] + f[12] + f[14]
        rho = (halo(10) + more) + (sum_e + sum_w)
        jx = sum_e - sum_w
        jy = (halo(11) + more_y) + ((f[7] - f[8]) + (f[10] - f[9]))
        jz = (halo(12) + more_z) + ((f[11] - f[12]) + (f[14] - f[13]))
        put(relax(rho, jx, jy, jz, f, entering), x)

    rows_of = (19, NZ, width, LANES)
    half = width // 2
    stores = [
        pltpu.make_async_copy(
            out_ref.reshape(rows_of).at[:, :, a : a + half], out_hbm.reshape(rows_of).at[:, :, a : a + half], sem_out.at[i]
        )
        for i, a in enumerate((0, half))
    ]
    for x in range(width):
        edge = beyond(pairs1, x)
        f = [insert(arrived(q, x), q, edge) for q in range(19)]
        post = relax(*moments(f), f, range(19))
        put(post, x)
        if x == half:
            stores[0].start()
    stores[1].start()
    for store in stores:
        store.wait()


def per_device(populations, le_cells, le_weight):
    width = populations.shape[2]
    height = populations.shape[3]
    flows = lax.axis_size("flow")
    shears = lax.axis_size("shear")
    assert populations.shape[:2] == (19, NZ) and height == LANES
    assert width * GAP == HALF and shears >= 4 and shears % 2 == 0 and flows >= 4 and flows & (flows - 1) == 0
    f32 = jnp.float32
    f = populations.reshape(19, NZ * width, height)
    vmem = pl.BlockSpec(memory_space=pltpu.VMEM)
    anyspace = pl.BlockSpec(memory_space=pl.ANY)
    hbm = pl.BlockSpec(memory_space=pltpu.HBM)
    smem = pl.BlockSpec(memory_space=pltpu.SMEM)
    params = pltpu.CompilerParams(vmem_limit_bytes=32 * 1024 * 1024)

    def body(kernel, *fixed):
        return lambda *refs: kernel(*fixed, *refs)

    def vregs(*counts):
        return jax.ShapeDtypeStruct((*counts, NZ, LANES), f32)

    def call(name, kernel, outs, *arrays):
        return pl.pallas_call(
            kernel, out_shape=outs, in_specs=[vmem] * len(arrays),
            out_specs=[vmem] * len(outs) if isinstance(outs, list) else vmem,
            compiler_params=params, name=name,
        )(*arrays)

    def swap(x, axis, partner):
        return lax.ppermute(x, axis, [(i, partner(i)) for i in range(lax.axis_size(axis))])

    side, gap, own, near, far = pl.pallas_call(
        body(pack_kernel, shears, width),
        out_shape=[vregs(2), vregs(2), vregs(2), vregs(13), vregs(13)],
        in_specs=[anyspace],
        out_specs=[vmem] * 5,
        scratch_shapes=[pltpu.VMEM((19, NZ * width, LANES), f32), pltpu.SemaphoreType.DMA((2,))],
        compiler_params=pltpu.CompilerParams(vmem_limit_bytes=55400000),
        name="pack",
    )(f)
    side = swap(side, "shear", lambda i: i ^ 1)
    gap = swap(gap, "shear", lambda i: (i - 1 + i % 2 * 2) % shears)
    mine = call("block", block_kernel, vregs(1, 3), gap, own)
    near, far = call("message", message_kernel, [vregs(16), vregs(16)], near, far, side, own)
    from_far = swap(far, "flow", lambda i: (i - 1 + i % 2 * 2) % flows)
    *early, last = gather_order(flows)
    for apart in early:
        theirs = swap(mine, "flow", lambda i: i ^ apart)
        mine = call("join", body(join_kernel, apart), vregs(2 * mine.shape[0], 3), mine, theirs)
    theirs = swap(mine, "flow", lambda i: i ^ last)
    from_near = swap(near, "flow", lambda i: i ^ 1)
    streamed = pl.pallas_call(
        body(local_kernel, width),
        out_shape=jax.ShapeDtypeStruct((19, width + 2, NZ, LANES), f32),
        in_specs=[vmem],
        out_specs=vmem,
        compiler_params=params,
        cost_estimate=pl.CostEstimate(flops=8_000_000, bytes_accessed=2_700_000, transcendentals=0),
        name="local",
    )(f)
    out = pl.pallas_call(
        body(finish_kernel, flows, shears, width),
        out_shape=jax.ShapeDtypeStruct((19, NZ * width, LANES), f32),
        in_specs=[vmem] * 9,
        out_specs=anyspace,
        scratch_shapes=[
            pltpu.VMEM((19, NZ * width, LANES), f32),
            pltpu.SemaphoreType.DMA((2,)),
        ],
        compiler_params=params,
        name="finish",
    )(le_cells, le_weight, streamed, mine, theirs, side, own, from_far, from_near)
    return out.reshape(populations.shape)


def solution(mesh):
    return jax.shard_map(
        per_device,
        mesh=mesh,
        in_specs=(P(None, None, "flow", "shear"), P(), P()),
        out_specs=P(None, None, "flow", "shear"),
        check_vma=False,
    )
```
